256 devices in a mesh: ctx: 32 (over y, x, z_hi), tp: 8 (over z_lo, core).
Axes of the slice: x: 4, y: 4, z: 8 (z_hi: 2, z_lo: 4; z = z_hi * 4 + z_lo), core: 2. Of those that a mesh axis runs over, the one named last changes fastest.
Arguments:
- segment_ordering: int32 [64], replicated, may hold values from 0 to 63, as said below
- attention_input: bfloat16 [4096, 8192], P('ctx', 'tp'), may hold values from -6 to 6
- residual: bfloat16 [4096, 3584], P(('ctx', 'tp')), may hold values from -6 to 6
- queries: bfloat16 [4096, 12288], P('ctx', 'tp'), may hold values from -120 to 120
- output_weight: bfloat16 [8192, 3584], P('tp'), may hold values from -0.0625 to 0.0625
- adapter_down_factor: bfloat16 [8192, 256], P('tp'), may hold values from -0.0625 to 0.0625
- adapter_up_factor: bfloat16 [256, 3584], replicated, may hold values from -0.375 to 0.375
- input_norm_gain: bfloat16 [3584], replicated, may hold values from 0.099609375 to 1.8984375
- latent_key_weight: bfloat16 [3584, 576], P('ctx'), may hold values from -0.09375 to 0.09375
- latent_norm_gain: bfloat16 [512], replicated, may hold values from 0.099609375 to 1.8984375
- latent_up_weight: bfloat16 [512, 16384], P(None, 'tp'), may hold values from -0.25 to 0.25
Outputs:
- hidden: bfloat16 [4096, 3584], P(('ctx', 'tp'))
- attn: bfloat16 [4096, 8192], P('ctx', 'tp')
The draws below stay inside these ranges and needn't reach their ends.
Inputs may be any that keep to these rules, and one draw needn't show every extreme that they name: `segment_ordering`: entries 2 i and 2 i + 1 (the segments stored by one index of ctx) sum to 63, and every segment number appears once.
All inputs are finite; a program needn't handle non-finite values.
Results may differ from the reference program's by a relative error of at most 0.04.
Values may be sent and summed in bfloat16 or wider, within the bound.
No kernel may reach another device: no remote copies, remote signals or barrier semaphores. Data moves between devices by JAX's collectives and lax.ppermute only.
A program may use at most 64 MiB of HBM per device.

```python
import math
import jax
import jax.numpy as jnp
from jax import lax

RESIDUAL_WIDTH = 3584
LATENT = 512
ROPE = 64
NOPE = 128
VDIM = 128
ADAPTER_RANK = 256
HEADS = 64
INPUT_WIDTH = 8192
TOKENS = 4096
SEGLEN = 64
SEGMENTS = 64


def draw_segment_ordering(key, part):
    key = jax.random.fold_in(key, 3)
    key_pairs, key_flip = jax.random.split(key)
    halves = SEGMENTS // 2
    pairing = jax.random.permutation(key_pairs, halves).astype(jnp.int32)
    flipped = jax.random.randint(key_flip, (halves,), 0, 2)
    leading = jnp.where(flipped == 1, SEGMENTS - 1 - pairing, pairing)
    trailing = SEGMENTS - 1 - leading
    return jnp.stack([leading, trailing], axis=1).reshape(SEGMENTS).astype(jnp.int32)


def draw_queries(key, part):
    key = jax.random.fold_in(key, 7)
    key_base = jax.random.fold_in(key, 0)
    shape = (TOKENS, HEADS * (NOPE + ROPE))
    values = 2.5 * jax.random.normal(key_base, shape, jnp.float32)
    return jnp.clip(values, -120.0, 120.0).astype(jnp.bfloat16)


def block_scale(own_key, dims, cuts, low, top_value):
    factor_of, own = 1.0, jax.random.fold_in(own_key, 6)
    for dim, blocks in cuts:
        heights = jnp.exp(jax.random.uniform(jax.random.fold_in(own, dim), (blocks,), jnp.float32, low / len(cuts), top_value / len(cuts)))
        factor_of = factor_of * jnp.repeat(heights, dims[dim] // blocks).reshape([-1 if axis == dim else 1 for axis in range(len(dims))])
    return factor_of


def centred(own_key, extent, width, bound, cuts=(), kind=jnp.bfloat16):
    array = jax.random.normal(own_key, extent, jnp.float32) * width
    if len(cuts) > 0:
        array = block_scale(own_key, extent, cuts, -0.22, 0.18) * array
    return jnp.clip(array, min=-bound, max=bound).astype(kind)


def setup_inputs(seed: int = 0) -> dict:
    arg_keys = jax.random.split(jax.random.key(seed), 12)
    return {
        "segment_ordering": draw_segment_ordering(jax.random.fold_in(arg_keys[11], 71), 0),
        "attention_input": centred(arg_keys[1], (TOKENS, INPUT_WIDTH), 1.0, 6.0, ((0, 32), (1, 8))),
        "residual": centred(arg_keys[2], (TOKENS, RESIDUAL_WIDTH), 1.0, 6.0, ((0, 256),)),
        "queries": draw_queries(jax.random.fold_in(arg_keys[11], 71), 0),
        "output_weight": centred(arg_keys[4], (INPUT_WIDTH, RESIDUAL_WIDTH), INPUT_WIDTH ** -0.5, 0.0625, ((0, 8),)),
        "adapter_down_factor": centred(arg_keys[5], (INPUT_WIDTH, ADAPTER_RANK), INPUT_WIDTH ** -0.5, 0.0625, ((0, 8),)),
        "adapter_up_factor": centred(arg_keys[6], (ADAPTER_RANK, RESIDUAL_WIDTH), ADAPTER_RANK ** -0.5, 0.375),
        "input_norm_gain": jnp.clip(1.0 + 0.18 * jax.random.normal(arg_keys[7], (RESIDUAL_WIDTH,), jnp.float32), 0.099609375, 1.8984375).astype(jnp.bfloat16),
        "latent_key_weight": centred(arg_keys[8], (RESIDUAL_WIDTH, LATENT + ROPE), RESIDUAL_WIDTH ** -0.5, 0.09375, ((0, 32),)),
        "latent_norm_gain": jnp.clip(1.0 + 0.18 * jax.random.normal(arg_keys[9], (LATENT,), jnp.float32), 0.099609375, 1.8984375).astype(jnp.bfloat16),
        "latent_up_weight": centred(arg_keys[10], (LATENT, HEADS * (NOPE + VDIM)), LATENT ** -0.5, 0.25, ((1, 8),)),
    }


def rms_scaled(values, gain):
    mean_square = lax.optimization_barrier(jnp.mean(values * values, axis=-1, keepdims=True))
    return values * lax.rsqrt(mean_square + 1e-06) * gain.astype(jnp.float32)

def rotate(values, places):
    half_width = values.shape[-1] // 2
    ladder = jnp.arange(half_width, dtype=jnp.float32)
    inverse = jnp.exp(ladder * (-2.0 * math.log(10000.0) / values.shape[-1]))
    angles = places.astype(jnp.float32)[:, None] * inverse[None, :]
    cosine = jnp.cos(angles)
    sine = jnp.sin(angles)
    first = values[:, :half_width]
    second = values[:, half_width:]
    return jnp.concatenate([first * cosine - second * sine, first * sine + second * cosine], axis=1)

def reference(segment_ordering, attention_input, residual, queries, output_weight, adapter_down_factor, adapter_up_factor, input_norm_gain, latent_key_weight, latent_norm_gain, latent_up_weight):
    rows = jnp.arange(TOKENS, dtype=jnp.int32)
    places = segment_ordering[rows // SEGLEN].astype(jnp.int32) * SEGLEN + rows % SEGLEN
    down_product = jnp.dot(attention_input, adapter_down_factor, preferred_element_type=jnp.float32)
    base = jnp.dot(attention_input, output_weight, preferred_element_type=jnp.float32)
    adapter_delta = jnp.dot(down_product, adapter_up_factor.astype(jnp.float32), precision=lax.Precision.HIGHEST)
    hidden = (residual.astype(jnp.float32) + base + adapter_delta).astype(jnp.bfloat16)
    normed = rms_scaled(hidden.astype(jnp.float32), input_norm_gain).astype(jnp.bfloat16)
    latent = jnp.dot(normed, latent_key_weight, preferred_element_type=jnp.float32)
    compressed = rms_scaled(latent[:, :LATENT], latent_norm_gain)
    key_rope = rotate(latent[:, LATENT:], places)
    kv_rows = jnp.concatenate([compressed, key_rope], axis=1).astype(jnp.bfloat16)
    lifted = jnp.dot(kv_rows[:, :LATENT], latent_up_weight, preferred_element_type=jnp.float32).astype(jnp.bfloat16)
    lifted = lifted.reshape(TOKENS, HEADS, NOPE + VDIM)
    shared = jnp.broadcast_to(kv_rows[:, None, LATENT:], (TOKENS, HEADS, ROPE))
    keys = jnp.transpose(jnp.concatenate([lifted[:, :, :NOPE], shared], axis=2), (1, 0, 2))
    values = jnp.transpose(lifted[:, :, NOPE:], (1, 0, 2))
    query_heads = jnp.transpose(queries.reshape(TOKENS, HEADS, NOPE + ROPE), (1, 0, 2))
    visible = places[None, :] <= places[:, None]
    scale = 1.0 / math.sqrt(NOPE + ROPE)

    def one_head(operands):
        query_one, key_one, value_one = operands
        scores = jnp.dot(query_one, key_one.T, preferred_element_type=jnp.float32) * scale
        masked = jnp.where(visible, scores, -1e+30)
        top_score = lax.optimization_barrier(jnp.max(masked, axis=1, keepdims=True))
        weights = jnp.where(visible, jnp.exp(masked - top_score), 0.0)
        totals = lax.optimization_barrier(jnp.sum(weights, axis=1, keepdims=True))
        mixed = jnp.dot(weights.astype(jnp.bfloat16), value_one, preferred_element_type=jnp.float32)
        return (mixed / totals).astype(jnp.bfloat16)
    outputs = lax.map(one_head, (query_heads, keys, values))
    attn = jnp.transpose(outputs, (1, 0, 2)).reshape(TOKENS, HEADS * VDIM)
    return (hidden, attn)
```

```python
import functools
import math

import jax
import jax.numpy as jnp
from jax import lax
from jax.experimental import pallas as pl
from jax.experimental.pallas import tpu as pltpu
from jax.sharding import Mesh, PartitionSpec as P

LATENT = 512
ROPE = 64
NOPE = 128
VDIM = 128
HEADS = 8
WIDE = 640
COLS = 896
BF = jnp.bfloat16
F32 = jnp.float32
MIB = 1 << 20
AXES = ("y", "x", "zh", "zl", "core")
SIZES = (4, 4, 2, 4, 2)
ORDER = (2, 1, 3, 0)


def dot(a, b):
    return jnp.dot(a, b, preferred_element_type=F32)


def shift(value, axis, k):
    return lax.ppermute(value, axis, [(i, (i + k) % 4) for i in range(4)])


def swap(value, axis):
    return lax.ppermute(value, axis, [(0, 1), (1, 0)])


def flat(y, x, zh, zl, core):
    return (((y * 4 + x) * 2 + zh) * 4 + zl) * 2 + core


def transposed_blocks(value):
    perm = []
    for y in range(4):
        for x in range(4):
            for zh in range(2):
                for zl in range(4):
                    for core in range(2):
                        perm.append((flat(zl, x, core, y, zh), flat(y, x, zh, zl, core)))
    return lax.ppermute(value, AXES, perm)


def params(mib):
    return pltpu.CompilerParams(vmem_limit_bytes=mib * MIB)


def shape(dims, dtype=BF):
    return jax.ShapeDtypeStruct(dims, dtype)


def project_kernel(s, x_ref, ad_ref, wo_ref, au_ref, res_ref, send_ref, keep_ref, xr, d3):
    core, zl = s[4], s[3]

    @pl.when(pl.program_id(0) == 0)
    def _():
        xr[0:64, :] = x_ref[:, 1 - core].reshape(64, 1024)
        xr[64:128, :] = x_ref[:, core].reshape(64, 1024)
        down = dot(xr[...], ad_ref[...])
        high = down.astype(BF)
        rest = down - high.astype(F32)
        middle = rest.astype(BF)
        d3[0] = high
        d3[1] = middle
        d3[2] = (rest - middle.astype(F32)).astype(BF)

    acc = dot(xr[...], wo_ref[...])
    for piece in range(3):
        acc += dot(d3[piece], au_ref[...])
    send_ref[0] = acc[:64].astype(BF)
    keep_ref[0] = acc[64:]
    rows = pl.ds(pl.multiple_of(zl * 16, 16), 16)
    keep_ref[0, rows, :] = keep_ref[0, rows, :] + res_ref[...].astype(F32)


def project(scalars, x4, down, weight, up, residual):
    block = lambda i, s: (0, s[8 + i])
    return pl.pallas_call(
        project_kernel,
        grid_spec=pltpu.PrefetchScalarGridSpec(
            num_scalar_prefetch=1,
            grid=(4,),
            in_specs=[
                pl.BlockSpec((4, 2, 16, 1024), lambda i, s: (0, 0, 0, 0)),
                pl.BlockSpec((1024, 256), lambda i, s: (0, 0)),
                pl.BlockSpec((1024, COLS), block),
                pl.BlockSpec((256, COLS), block),
                pl.BlockSpec((16, COLS), block),
            ],
            out_specs=[pl.BlockSpec((1, 64, COLS), lambda i, s: (i, 0, 0))] * 2,
            scratch_shapes=[pltpu.VMEM((128, 1024), BF), pltpu.VMEM((3, 128, 256), BF)],
        ),
        out_shape=[shape((4, 64, COLS)), shape((4, 64, COLS), F32)],
        compiler_params=params(24),
        name="project",
    )(scalars, x4, down, weight, up, residual)


def pair_sum_kernel(keep_ref, got_ref, *outs):
    for k in range(3):
        outs[k][...] = (keep_ref[k] + got_ref[k].astype(F32)).astype(BF)


def pair_sum(keep, got):
    spec = pl.BlockSpec((3, 64, COLS), lambda i: (0, 0, 0))
    return pl.pallas_call(
        pair_sum_kernel,
        grid=(1,),
        in_specs=[spec, spec],
        out_specs=[pl.BlockSpec((64, COLS), lambda i: (0, 0))] * 3,
        out_shape=[shape((64, COLS))] * 3,
        compiler_params=params(16),
        name="pair_sum",
    )(keep, got)


def assemble_kernel(s, *refs):
    out_ref = refs[8]
    x, core = s[1], s[4]
    out_ref[:, 512:] = jnp.zeros((COLS, WIDE - 512), BF)
    for k in range(4):
        for other in range(2):
            zh = (core + other) % 2
            row = pl.multiple_of(((x + k) % 4) * 224 + zh * 112, 16)
            out_ref[pl.ds(row, 112), 0:576] = refs[4 * other + k][...]


def assemble(scalars, blocks):
    return pl.pallas_call(
        assemble_kernel,
        in_specs=[pl.BlockSpec(memory_space=pltpu.SMEM)] + [pl.BlockSpec(memory_space=pltpu.VMEM)] * 8,
        out_specs=pl.BlockSpec(memory_space=pltpu.VMEM),
        out_shape=shape((COLS, WIDE)),
        compiler_params=params(16),
        name="assemble",
    )(scalars, *blocks)


def latent_kernel(s, keep_ref, got_ref, r1, r2, r3, gain_ref, w_ref, part_ref, h0, h1, h2, h3, hid):
    zl = s[3]
    total = keep_ref[0] + got_ref[0].astype(F32) + r1[...].astype(F32) + r2[...].astype(F32) + r3[...].astype(F32)
    hidden = total.astype(BF)
    hid[...] = hidden
    for k, out in enumerate((h0, h1, h2, h3)):
        out[...] = hid[pl.ds(pl.multiple_of(((zl + k) % 4) * 16, 16), 16), :]
    wide = hidden.astype(F32)
    squares = jnp.sum(wide * wide, axis=1, keepdims=True)
    part = dot((wide * gain_ref[...].astype(F32)).astype(BF), w_ref[...])
    lane = lax.broadcasted_iota(jnp.int32, (64, 128), 1)
    high = squares.astype(BF).astype(F32)
    tail = jnp.where(lane == 64, high, jnp.where(lane == 65, squares - high, part[:, 512:]))
    part_ref[:, :512] = part[:, :512].astype(BF)
    part_ref[:, 512:] = tail.astype(BF)


def latent_part(scalars, keep, got, r1, r2, r3, gain, weight):
    own = pl.BlockSpec((1, 64, COLS), lambda i, s: (3, 0, 0))
    block = pl.BlockSpec((64, COLS), lambda i, s: (0, 0))
    small = pl.BlockSpec((16, COLS), lambda i, s: (0, 0))
    return pl.pallas_call(
        latent_kernel,
        grid_spec=pltpu.PrefetchScalarGridSpec(
            num_scalar_prefetch=1,
            grid=(1,),
            in_specs=[
                own,
                own,
                block,
                block,
                block,
                pl.BlockSpec((1, COLS), lambda i, s: (0, s[3])),
                pl.BlockSpec((COLS, WIDE), lambda i, s: (0, 0)),
            ],
            out_specs=[pl.BlockSpec((64, WIDE), lambda i, s: (0, 0))] + [small] * 4,
            scratch_shapes=[pltpu.VMEM((64, COLS), BF)],
        ),
        out_shape=[shape((64, WIDE))] + [shape((16, COLS))] * 4,
        compiler_params=params(24),
        name="latent_part",
    )(scalars, keep, got, r1, r2, r3, gain, weight)


def rows_kernel(p0, p1, p2, p3, cos_ref, sin_ref, gain_ref, out_ref):
    total = p0[...].astype(F32) + p1[...].astype(F32) + p2[...].astype(F32) + p3[...].astype(F32)
    tail = total[:, 512:]
    inverse = lax.rsqrt((tail[:, 64:65] + tail[:, 65:66]) / 3584.0 + 1e-06)
    latent = total[:, :512] * inverse
    mean_square = jnp.mean(latent * latent, axis=1, keepdims=True)
    out_ref[:, :512] = (latent * lax.rsqrt(mean_square + 1e-06) * gain_ref[...].astype(F32)).astype(BF)
    rope = tail[:, :64] * inverse
    swapped = jnp.concatenate([rope[:, 32:], rope[:, :32]], axis=1)
    rotated = rope * cos_ref[...] + swapped * sin_ref[...]
    out_ref[:, 512:] = jnp.concatenate([rotated, jnp.zeros((64, 64), F32)], axis=1).astype(BF)


def kv_rows(parts, cosine, sine, gain):
    return pl.pallas_call(
        rows_kernel,
        out_shape=shape((64, WIDE)),
        compiler_params=params(16),
        name="kv_rows",
    )(*parts, cosine, sine, gain)


def attend_kernel(heads, s, seg, q0, q1, q2, q3, *refs):
    keys = refs[:8]
    up_ref = refs[8]
    outs = refs[9:13]
    kv, bias, stats = refs[13:]
    step = pl.program_id(0)
    y, x, zh, core = s[0], s[1], s[2], s[4]
    factor = math.log2(math.e) / math.sqrt(NOPE + ROPE)

    @pl.when(step == 0)
    def _():
        for k in range(4):
            for other in range(2):
                kv[k * 256 + other * 128 : k * 256 + other * 128 + 128, :] = keys[4 * other + k][...]
        lane = lax.broadcasted_iota(jnp.int32, (1, 1024), 1)
        group = lane // 256 * 4 + (lane // 64) % 2 * 2 + (lane // 32) % 2
        segment = jnp.zeros((1, 1024), jnp.int32)
        for k in range(4):
            for a in range(2):
                for half in range(2):
                    ctx = ((y + k) % 4) * 8 + x * 2 + (zh + a) % 2
                    segment = jnp.where(group == k * 4 + a * 2 + half, seg[2 * ctx + half], segment)
        side = ((lane // 128) % 2 + core) % 2
        place = segment * 64 + (lane // 16) % 2 * 32 + side * 16 + lane % 16
        row = lax.broadcasted_iota(jnp.int32, (64, 1024), 0)
        for j in range(4):
            ctx = y * 8 + ((x + j) % 4) * 2 + zh
            for half in range(2):
                mine = row + seg[2 * ctx + half] * 64
                start = j * 128 + half * 64
                bias[start : start + 64, :] = jnp.where(place <= mine, 0.0, -1e30)
        stats[...] = jnp.zeros_like(stats)

    lane = lax.broadcasted_iota(jnp.int32, (128, 128), 1)
    for side in range(2):
        lifted = dot(kv[:, :LATENT], up_ref[:, side * 256 : side * 256 + 256]).astype(BF)
        key = jnp.concatenate([lifted[:, :NOPE], kv[:, LATENT:]], axis=1)
        value = lifted[:, NOPE:]
        head = 2 * step + side
        for j, q in enumerate((q0, q1, q2, q3)):
            first = side * 192
            query = jnp.concatenate([q[:, first : first + 192], jnp.zeros((128, 64), BF)], axis=1)
            scores = lax.dot_general(query, key, (((1,), (1,)), ((), ())), preferred_element_type=F32)
            scores = scores + bias[j * 128 : j * 128 + 128, :]
            top = jnp.max(scores, axis=1, keepdims=True)
            weights = jnp.exp2((scores - top) * factor)
            total = jnp.sum(weights, axis=1, keepdims=True)
            mixed = dot(weights.astype(BF), value) / total
            outs[j][:, pl.ds(pl.multiple_of(head * 128, 128), 128)] = mixed.astype(BF)
            level = top * factor + jnp.log2(total)
            high = level.astype(BF).astype(F32)
            middle = (level - high).astype(BF).astype(F32)
            low = level - high - middle
            stats[j] = stats[j] + jnp.where(
                lane == head,
                high,
                jnp.where(lane == head + 8, middle, jnp.where(lane == head + 16, low, 0.0)),
            )

    @pl.when(step == pl.num_programs(0) - 1)
    def _():
        for j in range(4):
            outs[j][:, heads * 128 :] = stats[j].astype(BF)


def attend(scalars, seg, queries, keys, up, first_pair, pairs):
    heads = 2 * pairs
    width = heads * 128 + 128
    return pl.pallas_call(
        functools.partial(attend_kernel, heads),
        grid_spec=pltpu.PrefetchScalarGridSpec(
            num_scalar_prefetch=2,
            grid=(pairs,),
            in_specs=[pl.BlockSpec((128, 384), lambda i, s, g: (0, i + first_pair))] * 4
            + [pl.BlockSpec((128, WIDE), lambda i, s, g: (0, 0))] * 8
            + [pl.BlockSpec((LATENT, 512), lambda i, s, g: (0, i + first_pair))],
            out_specs=[pl.BlockSpec((128, width), lambda i, s, g: (0, 0))] * 4,
            scratch_shapes=[
                pltpu.VMEM((1024, WIDE), BF),
                pltpu.VMEM((512, 1024), F32),
                pltpu.VMEM((4, 128, 128), F32),
            ],
        ),
        out_shape=[shape((128, width))] * 4,
        compiler_params=params(48),
        name="attend",
    )(scalars, seg, *queries, *keys, up)


def merge_kernel(heads, *refs):
    out_ref = refs[-1]
    for part in range(2):
        group = refs[4 * part : 4 * part + 4]
        for head in range(heads):
            levels = []
            for ref in group:
                stat = ref[:, heads * 128 :].astype(F32)
                levels.append(stat[:, head : head + 1] + stat[:, head + 8 : head + 9] + stat[:, head + 16 : head + 17])
            top = functools.reduce(jnp.maximum, levels)
            scales = [jnp.exp2(level - top) for level in levels]
            total = sum(scales[1:], scales[0])
            mixed = sum(
                ref[:, head * 128 : head * 128 + 128].astype(F32) * (scale / total)
                for ref, scale in zip(group, scales)
            )
            column = (part * heads + head) * 128
            out_ref[:, column : column + 128] = mixed.astype(BF)


def merge(first, second):
    return pl.pallas_call(
        functools.partial(merge_kernel, 4),
        out_shape=shape((128, HEADS * VDIM)),
        compiler_params=params(16),
        name="merge",
    )(*first, *second)


def hidden_kernel(s, h0, h1, h2, h3, out_ref):
    zl = s[3]
    for k, ref in enumerate((h0, h1, h2, h3)):
        column = pl.multiple_of(((zl + 4 - k) % 4) * COLS, 128)
        out_ref[:, pl.ds(column, COLS)] = ref[...]


def hidden_rows(scalars, blocks):
    return pl.pallas_call(
        hidden_kernel,
        in_specs=[pl.BlockSpec(memory_space=pltpu.SMEM)] + [pl.BlockSpec(memory_space=pltpu.VMEM)] * 4,
        out_specs=pl.BlockSpec(memory_space=pltpu.VMEM),
        out_shape=shape((16, 4 * COLS)),
        compiler_params=params(16),
        name="hidden_rows",
    )(scalars, *blocks)


def rotary_tables(segment_ordering, ctx, core):
    row = jnp.arange(64, dtype=jnp.int32)
    token = row // 16 * 32 + core * 16 + row % 16
    pair = lax.dynamic_slice_in_dim(segment_ordering, 2 * ctx, 2)
    places = jnp.where(token < 64, pair[0], pair[1]) * 64 + token % 64
    ladder = jnp.arange(ROPE // 2, dtype=F32)
    inverse = jnp.exp(ladder * (-2.0 * math.log(10000.0) / ROPE))
    angles = places.astype(F32)[:, None] * inverse[None, :]
    cosine, sine = jnp.cos(angles), jnp.sin(angles)
    return jnp.concatenate([cosine, cosine], axis=1), jnp.concatenate([-sine, sine], axis=1)


def body(
    segment_ordering,
    attention_input,
    residual,
    queries,
    output_weight,
    adapter_down_factor,
    adapter_up_factor,
    input_norm_gain,
    latent_key_weight,
    latent_norm_gain,
    latent_up_weight,
):
    y, x, zh, zl, core = (lax.axis_index(name) for name in AXES)
    scalars = jnp.stack([y, x, zh, zl, core, 0, 0, 0] + [(zl + k) % 4 for k in ORDER]).astype(jnp.int32)

    own = transposed_blocks(latent_key_weight)
    lined = [own] + [shift(own, "x", -k) for k in (1, 2, 3)]
    weight = assemble(scalars, lined + [swap(block, "core") for block in lined])
    asked = [queries] + [shift(queries, "x", -k) for k in (1, 2, 3)]
    cosine, sine = rotary_tables(segment_ordering, y * 8 + x * 2 + zh, core)

    send, keep = project(
        scalars,
        attention_input.reshape(4, 2, 16, 1024),
        adapter_down_factor,
        output_weight,
        adapter_up_factor,
        residual,
    )
    got = swap(send, "core")
    sums = pair_sum(keep, got)
    r2, r1, r3 = (shift(value, "zl", k) for value, k in zip(sums, ORDER))
    part, h0, h1, h2, h3 = latent_part(
        scalars, keep, got, r1, r2, r3, input_norm_gain.reshape(1, -1), weight
    )
    parts = [part] + [shift(part, "zl", k) for k in (1, 2, 3)]
    rows = kv_rows(parts, cosine, sine, latent_norm_gain.reshape(1, -1))
    both = jnp.concatenate([rows, swap(rows, "zh")], axis=0)
    column = [both] + [shift(both, "y", -k) for k in (1, 2, 3)]
    keys = column + [swap(value, "core") for value in column]

    hidden = hidden_rows(scalars, [h0] + [shift(h, "zl", k) for k, h in ((1, h1), (2, h2), (3, h3))])

    halves = []
    for first in (0, 2):
        partial = attend(scalars, segment_ordering, asked, keys, latent_up_weight, first, 2)
        halves.append([partial[0]] + [shift(partial[j], "x", j) for j in (1, 2, 3)])
    return hidden, merge(*halves)


def solution(mesh):
    split = Mesh(mesh.devices.reshape(SIZES), AXES)
    ctx, tp = ("y", "x", "zh"), ("zl", "core")
    in_specs = (
        P(),
        P(ctx, tp),
        P(ctx + tp, None),
        P(ctx, tp),
        P(tp, None),
        P(tp, None),
        P(),
        P(),
        P(ctx, None),
        P(),
        P(None, tp),
    )
    out_specs = (P(ctx + tp, None), P(ctx, tp))
    return jax.shard_map(body, mesh=split, in_specs=in_specs, out_specs=out_specs, check_vma=False)
```

```python
import functools
import math

import jax
import jax.numpy as jnp
from jax import lax
from jax.experimental import pallas as pl
from jax.experimental.pallas import tpu as pltpu
from jax.sharding import Mesh, PartitionSpec as P

LATENT = 512
ROPE = 64
NOPE = 128
VDIM = 128
HEADS = 8
WIDE = 640
MESSAGE = HEADS * VDIM + 128
COLS = 896
BF = jnp.bfloat16
F32 = jnp.float32
MIB = 1 << 20
AXES = ("y", "x", "zh", "zl", "core")
SIZES = (4, 4, 2, 4, 2)
ORDER = (2, 1, 3, 0)


def dot(a, b):
    return jnp.dot(a, b, preferred_element_type=F32)


def shift(value, axis, k):
    return lax.ppermute(value, axis, [(i, (i + k) % 4) for i in range(4)])


def swap(value, axis, bit=1, size=2):
    return lax.ppermute(value, axis, [(i, i ^ bit) for i in range(size)])


def flat(y, x, zh, zl, core):
    return (((y * 4 + x) * 2 + zh) * 4 + zl) * 2 + core


def turn(value, k):
    perm = []
    for x in range(4):
        for core in range(2):
            perm.append((x * 2 + core, (x + (k if core == 0 else -k)) % 4 * 2 + core))
    return lax.ppermute(value, ("x", "core"), perm)


def tie(*values):
    return lax.optimization_barrier(values)


def transposed_block(value):
    perm = []
    for y in range(4):
        for x in range(4):
            for zh in range(2):
                for zl in range(4):
                    for core in range(2):
                        perm.append((flat(zl, x, core, y, zh), flat(y, x, zh, zl, core)))
    return lax.ppermute(value, AXES, perm)


def coords(s):
    f = s[0]
    return f // 64, f // 16 % 4, f // 8 % 2, f // 2 % 4, f % 2


def params(mib):
    return pltpu.CompilerParams(vmem_limit_bytes=mib * MIB)


def shape(dims, dtype=BF):
    return jax.ShapeDtypeStruct(dims, dtype)


def project_kernel(s, x_hbm, ad_hbm, w_hbm, au_hbm, res_hbm, send_ref, keep_ref, x, ad, w, au, res, xr, kept, sem):
    _, _, _, zl, core = coords(s)
    columns = [pl.ds(pl.multiple_of((zl + k) % 4 * COLS, 128), COLS) for k in ORDER]

    def fetch(source, target, index):
        copy = pltpu.make_async_copy(source, target, sem.at[index])
        copy.start()
        return copy

    first = [fetch(x_hbm, x, 0), fetch(ad_hbm, ad, 1)]
    weights = [fetch(w_hbm.at[:, column], w.at[b], 4 + b) for b, column in enumerate(columns[:1])]
    second = [fetch(au_hbm, au, 2), fetch(res_hbm, res, 3)]
    weights += [fetch(w_hbm.at[:, column], w.at[b + 1], 5 + b) for b, column in enumerate(columns[1:])]
    for copy in first:
        copy.wait()
    xr[0:64, :] = x[:, 1 - core].reshape(64, 1024)
    xr[64:128, :] = x[:, core].reshape(64, 1024)
    down = dot(xr[...], ad[...])
    high = down.astype(BF)
    pieces = jnp.concatenate([high, (down - high.astype(F32)).astype(BF)], axis=0)
    rows = pl.ds(pl.multiple_of(zl * 16, 16), 16)
    for b, column in enumerate(columns):
        weights[b].wait()
        acc = dot(xr[...], w[b])
        if b == 0:
            for copy in second:
                copy.wait()
        adapter = dot(pieces, au[:, column])
        acc = acc + adapter[:128] + adapter[128:]
        send_ref[b] = acc[:64].astype(BF)
        kept[...] = acc[64:]
        kept[rows, :] = kept[rows, :] + res[:, column].astype(F32)
        keep_ref[b] = kept[...].astype(BF)


def project(scalars, *operands):
    return pl.pallas_call(
        project_kernel,
        in_specs=[pl.BlockSpec(memory_space=pltpu.SMEM)] + [pl.BlockSpec(memory_space=pltpu.HBM)] * 5,
        out_specs=[pl.BlockSpec(memory_space=pltpu.VMEM)] * 2,
        out_shape=[shape((4, 64, COLS))] * 2,
        scratch_shapes=[
            pltpu.VMEM((4, 2, 16, 1024), BF),
            pltpu.VMEM((1024, 256), BF),
            pltpu.VMEM((4, 1024, COLS), BF),
            pltpu.VMEM((256, 4 * COLS), BF),
            pltpu.VMEM((16, 4 * COLS), BF),
            pltpu.VMEM((128, 1024), BF),
            pltpu.VMEM((64, COLS), F32),
            pltpu.SemaphoreType.DMA((8,)),
        ],
        compiler_params=params(56),
        name="project",
    )(scalars, *operands)


def local(kernel, outs, mib, name, smem=0, vmem=0, scratch=()):
    space = lambda kind, n: [pl.BlockSpec(memory_space=kind)] * n
    out_specs = pl.BlockSpec(memory_space=pltpu.VMEM)
    return pl.pallas_call(
        kernel,
        in_specs=space(pltpu.SMEM, smem) + space(pltpu.VMEM, vmem),
        out_specs=[out_specs] * len(outs) if isinstance(outs, list) else out_specs,
        out_shape=outs,
        scratch_shapes=scratch,
        compiler_params=params(mib),
        name=name,
    )


def pair_sum_kernel(keep_ref, got_ref, *outs):
    for k, out in enumerate(outs):
        out[...] = (keep_ref[k].astype(F32) + got_ref[k].astype(F32)).astype(BF)


def pair_sum(keep, got, count):
    return local(pair_sum_kernel, [shape((64, COLS))] * count, 16, "pair_sum", vmem=2)(keep, got)


def pack_kernel(count, *refs):
    out_ref = refs[-1]
    start = 0
    for ref in refs[:count]:
        size = ref.shape[0]
        out_ref[start : start + size] = ref[...]
        start += size


def pack(blocks, after):
    dims = (sum(block.shape[0] for block in blocks),) + blocks[0].shape[1:]
    kernel = functools.partial(pack_kernel, len(blocks))
    return local(kernel, shape(dims), 16, "pack", vmem=len(blocks) + len(after))(*blocks, *after)


def assemble_kernel(s, own_ref, other_ref, out_ref):
    _, x, _, _, core = coords(s)
    out_ref[:, 512:] = jnp.zeros((COLS, WIDE - 512), BF)
    for k in range(4):
        for other, ref in enumerate((own_ref, other_ref)):
            zh = (core + other) % 2
            row = pl.multiple_of((x ^ k) * 224 + zh * 112, 16)
            out_ref[pl.ds(row, 112), 0:576] = ref[k]


def assemble(scalars, own, other):
    return local(assemble_kernel, shape((COLS, WIDE)), 16, "assemble", 1, 2)(scalars, own, other)


def tables_kernel(s, seg, cos_ref, sin_ref):
    y, x, zh, _, core = coords(s)
    ctx = y * 8 + x * 2 + zh
    row = lax.broadcasted_iota(jnp.int32, (64, ROPE), 0)
    lane = lax.broadcasted_iota(jnp.int32, (64, ROPE), 1)
    token = row // 16 * 32 + core * 16 + row % 16
    places = jnp.where(token < 64, seg[2 * ctx], seg[2 * ctx + 1]) * 64 + token % 64
    inverse = jnp.exp((lane % 32).astype(F32) * (-2.0 * math.log(10000.0) / ROPE))
    angles = places.astype(F32) * inverse
    cos_ref[...] = jnp.cos(angles)
    sine = jnp.sin(angles)
    sin_ref[...] = jnp.where(lane < 32, -sine, sine)


def tables(scalars, seg):
    return local(tables_kernel, [shape((64, ROPE), F32)] * 2, 16, "tables", 2)(scalars, seg)


def latent_kernel(s, keep_ref, got_ref, r1, r2, r3, gain_ref, w_ref, part_ref, h0, h1, h2, h3, hid):
    _, _, _, zl, _ = coords(s)
    total = sum(ref[...].astype(F32) for ref in (keep_ref.at[3], got_ref.at[3], r1, r2, r3))
    hidden = total.astype(BF)
    hid[...] = hidden
    for k, out in enumerate((h0, h1, h2, h3)):
        out[...] = hid[pl.ds(pl.multiple_of(((zl + k) % 4) * 16, 16), 16), :]
    wide = hidden.astype(F32)
    squares = jnp.sum(wide * wide, axis=1, keepdims=True)
    gain = gain_ref[:, pl.ds(pl.multiple_of(zl * COLS, 128), COLS)].astype(F32)
    part = dot((wide * gain).astype(BF), w_ref[...])
    lane = lax.broadcasted_iota(jnp.int32, (64, 128), 1)
    high = squares.astype(BF).astype(F32)
    tail = jnp.where(lane == 64, high, jnp.where(lane == 65, squares - high, part[:, 512:]))
    part_ref[:, :512] = part[:, :512].astype(BF)
    part_ref[:, 512:] = tail.astype(BF)


def latent_part(scalars, *operands):
    outs = [shape((64, WIDE))] + [shape((16, COLS))] * 4
    scratch = [pltpu.VMEM((64, COLS), BF)]
    return local(latent_kernel, outs, 16, "latent_part", 1, 7, scratch)(scalars, *operands)


def rows_kernel(p0, p1, p2, p3, cos_ref, sin_ref, gain_ref, out_ref):
    total = p0[...].astype(F32) + p1[...].astype(F32) + p2[...].astype(F32) + p3[...].astype(F32)
    tail = total[:, 512:]
    inverse = lax.rsqrt((tail[:, 64:65] + tail[:, 65:66]) / 3584.0 + 1e-06)
    latent = total[:, :512] * inverse
    mean_square = jnp.mean(latent * latent, axis=1, keepdims=True)
    out_ref[:, :512] = (latent * lax.rsqrt(mean_square + 1e-06) * gain_ref[...].astype(F32)).astype(BF)
    rope = tail[:, :64] * inverse
    swapped = jnp.concatenate([rope[:, 32:], rope[:, :32]], axis=1)
    rotated = rope * cos_ref[...] + swapped * sin_ref[...]
    out_ref[:, 512:] = jnp.concatenate([rotated, jnp.zeros((64, 64), F32)], axis=1).astype(BF)


def kv_rows(parts, cosine, sine, gain):
    return local(rows_kernel, shape((64, WIDE)), 16, "kv_rows", vmem=7)(*parts, cosine, sine, gain)


def lift_kernel(s, seg, *refs):
    keys = refs[:8]
    up_ref, key_ref, value_ref, kv = refs[8:]
    y, x, zh, _, _ = coords(s)
    for k in range(4):
        for a in range(2):
            ctx = ((y + k) % 4) * 8 + x * 2 + (zh + a) % 2
            first_upper = (seg[2 * ctx] > seg[2 * ctx + 1]).astype(jnp.int32)
            for half in range(2):
                upper = first_upper if half == 0 else 1 - first_upper
                for other in range(2):
                    row = pl.multiple_of(upper * 512 + (k * 2 + a) * 64 + other * 32, 32)
                    start = a * 64 + half * 32
                    kv[pl.ds(row, 32), :] = keys[4 * other + k][start : start + 32, :]
    ones = jnp.ones((1024, 128), BF)
    for head in range(HEADS):
        lifted = dot(kv[:, :LATENT], up_ref[:, head * 256 : head * 256 + 256]).astype(BF)
        key_ref[head, :, :NOPE] = lifted[:, :NOPE]
        key_ref[head, :, NOPE:] = kv[:, LATENT:]
        value_ref[head, :, :VDIM] = lifted[:, NOPE:]
        value_ref[head, :, VDIM:] = ones


def lift(scalars, seg, keys, up):
    outs = [shape((HEADS, 1024, 256))] * 2
    scratch = [pltpu.VMEM((1024, WIDE), BF)]
    return local(lift_kernel, outs, 24, "lift", 2, 9, scratch)(scalars, seg, *keys, up)


def stat_pieces(level, lane):
    high = level.astype(BF).astype(F32)
    middle = (level - high).astype(BF).astype(F32)
    return jnp.where(lane < 8, high, jnp.where(lane < 16, middle, level - high - middle))


def attend_kernel(chunks, s, seg, *refs):
    count = len(chunks)
    queries = refs[:count]
    key_ref, value_ref = refs[count : count + 2]
    outs = refs[count + 2 :]
    y, x, zh, _, core = coords(s)
    hops = (0, 1 + 2 * core, 2, 3 - 2 * core)
    factor = math.log2(math.e) / math.sqrt(NOPE + ROPE)
    lane = lax.broadcasted_iota(jnp.int32, (1, 512), 1)
    lower = jnp.zeros((1, 512), jnp.int32)
    upper = lower
    for k in range(4):
        for a in range(2):
            ctx = ((y + k) % 4) * 8 + x * 2 + (zh + a) % 2
            one, two = seg[2 * ctx], seg[2 * ctx + 1]
            lower = jnp.where(lane // 64 == k * 2 + a, jnp.minimum(one, two), lower)
            upper = jnp.where(lane // 64 == k * 2 + a, jnp.maximum(one, two), upper)
    inside = (lane // 16) % 2 * 32 + ((lane // 32) % 2 + core) % 2 * 16 + lane % 16
    row = lax.broadcasted_iota(jnp.int32, (64, 512), 0)
    low_rows, high_rows, low_bias, high_bias = [], [], [], []
    for chunk in chunks:
        ctx = y * 8 + ((x + hops[chunk]) % 4) * 2 + zh
        one, two = seg[2 * ctx], seg[2 * ctx + 1]
        flipped = (one > two).astype(jnp.int32)
        low_rows.append(pl.ds(pl.multiple_of(flipped * 64, 64), 64))
        high_rows.append(pl.ds(pl.multiple_of(64 - flipped * 64, 64), 64))
        low_bias.append(jnp.where(lower * 64 + inside <= row + jnp.minimum(one, two) * 64, 0.0, -1e30))
        high_bias.append(jnp.where(upper * 64 + inside <= row + jnp.maximum(one, two) * 64, 0.0, -1e30))
    low_bias = jnp.concatenate(low_bias, axis=0)
    high_bias = jnp.concatenate(high_bias, axis=0)
    rows = 64 * count
    stat_lane = lax.broadcasted_iota(jnp.int32, (2 * rows, 128), 1)
    stats = jnp.zeros((2 * rows, 128), F32)
    across = (((1,), (1,)), ((), ()))
    near, far = [], []
    for head in range(HEADS):
        column = slice(head * 192, head * 192 + 192)
        pieces = [q[r, column] for q, r in zip(queries, low_rows)] + [q[r, column] for q, r in zip(queries, high_rows)]
        query = jnp.concatenate([jnp.concatenate(pieces, axis=0), jnp.zeros((2 * rows, 64), BF)], axis=1)
        near.append(lax.dot_general(query, key_ref[head, :512, :], across, preferred_element_type=F32))
        high = lax.dot_general(query[rows:], key_ref[head, 512:, :], across, preferred_element_type=F32)
        far.append(high + high_bias)
    low = [scores[:rows] + low_bias for scores in near]
    mid = [scores[rows:] for scores in near]
    low_top = [jnp.max(scores, axis=1, keepdims=True) for scores in low]
    high_top = [jnp.max(jnp.maximum(a, b), axis=1, keepdims=True) for a, b in zip(mid, far)]
    weigh = lambda scores, top: jnp.exp2((scores - top) * factor).astype(BF)
    low = [weigh(a, t) for a, t in zip(low, low_top)]
    mid = [weigh(a, t) for a, t in zip(mid, high_top)]
    far = [weigh(a, t) for a, t in zip(far, high_top)]
    first = [dot(jnp.concatenate([a, b], axis=0), value_ref[h, :512, :]) for h, (a, b) in enumerate(zip(low, mid))]
    second = [dot(a, value_ref[h, 512:, :]) for h, a in enumerate(far)]
    for head in range(HEADS):
        both = jnp.concatenate([first[head][:rows], first[head][rows:] + second[head]], axis=0)
        top = jnp.concatenate([low_top[head], high_top[head]], axis=0)
        mixed = (both[:, :VDIM] / both[:, VDIM:]).astype(BF)
        level = top * factor + jnp.log2(both[:, VDIM:])
        stats = jnp.where(stat_lane % 8 == head, level, stats)
        for c in range(count):
            column = slice(head * 128, head * 128 + 128)
            outs[c][low_rows[c], column] = mixed[64 * c : 64 * c + 64]
            outs[c][high_rows[c], column] = mixed[rows + 64 * c : rows + 64 * c + 64]
    stats = jnp.where(stat_lane < 24, stat_pieces(stats, stat_lane), 0.0).astype(BF)
    for c in range(count):
        outs[c][low_rows[c], HEADS * 128 :] = stats[64 * c : 64 * c + 64]
        outs[c][high_rows[c], HEADS * 128 :] = stats[rows + 64 * c : rows + 64 * c + 64]


def attend(chunks, scalars, seg, queries, lifted):
    kernel = functools.partial(attend_kernel, chunks)
    outs = [shape((128, MESSAGE))] * len(chunks)
    return local(kernel, outs, 32, "attend", 2, len(chunks) + 2)(scalars, seg, *queries, *lifted)


def spread_levels(ref, width, group):
    row = lax.broadcasted_iota(jnp.int32, (128, width), 0)
    lane = lax.broadcasted_iota(jnp.int32, (128, width), 1)
    picks = (row < 24) & (row % 8 == (lane // group) % 8)
    return dot(ref[:, HEADS * 128 :], picks.astype(F32).astype(BF))


def merged(refs):
    levels = [spread_levels(ref, 1024, 128) for ref in refs]
    top = functools.reduce(jnp.maximum, levels)
    scales = [jnp.exp2(level - top) for level in levels]
    mixed = sum(ref[:, : HEADS * 128].astype(F32) * scale for ref, scale in zip(refs, scales))
    return (mixed / sum(scales[1:], scales[0])).astype(BF)


def relay_kernel(got_ref, own_ref, out_ref):
    refs = (got_ref, own_ref)
    out_ref[:, : HEADS * 128] = merged(refs)
    one, two = [spread_levels(ref, 128, 1) for ref in refs]
    top = jnp.maximum(one, two)
    level = top + jnp.log2(jnp.exp2(one - top) + jnp.exp2(two - top))
    lane = lax.broadcasted_iota(jnp.int32, (128, 128), 1)
    out_ref[:, HEADS * 128 :] = jnp.where(lane < 24, stat_pieces(level, lane), 0.0).astype(BF)


def relay(got, own):
    return local(relay_kernel, shape((128, MESSAGE)), 16, "relay", vmem=2)(got, own)


def merge_kernel(a_ref, b_ref, c_ref, out_ref):
    out_ref[...] = merged((a_ref, b_ref, c_ref))


def merge(a, b, c):
    return local(merge_kernel, shape((128, HEADS * VDIM)), 16, "merge", vmem=3)(a, b, c)


def hidden_kernel(s, h0, h1, h2, h3, out_ref):
    _, _, _, zl, _ = coords(s)
    for k, ref in enumerate((h0, h1, h2, h3)):
        column = pl.multiple_of(((zl + 4 - k) % 4) * COLS, 128)
        out_ref[:, pl.ds(column, COLS)] = ref[...]


def hidden_rows(scalars, blocks):
    return local(hidden_kernel, shape((16, 4 * COLS)), 16, "hidden_rows", 1, 4)(scalars, *blocks)


def body(
    segment_ordering,
    attention_input,
    residual,
    queries,
    output_weight,
    adapter_down_factor,
    adapter_up_factor,
    input_norm_gain,
    latent_key_weight,
    latent_norm_gain,
    latent_up_weight,
):
    scalars = lax.axis_index(AXES).astype(jnp.int32).reshape(1)
    near, away, far, back = 0, 1, 2, 3

    block = transposed_block(latent_key_weight)[None]
    send, keep = project(
        scalars,
        attention_input.reshape(4, 2, 16, 1024),
        adapter_down_factor,
        output_weight,
        adapter_up_factor,
        residual,
    )
    block, send = tie(block, send)
    got = swap(send, "core")
    blocks = [block] + [swap(block, "x", k, 4) for k in (1, 2, 3)]
    sums = pair_sum(keep, got, 3)
    r2, r1, r3 = (shift(value, "zl", k) for value, k in zip(sums, ORDER))
    four = pack(blocks, (r1, r2, r3))
    weight = assemble(scalars, four, swap(four, "core"))
    q_far, q_back = shift(queries, "x", 2), turn(queries, 1)
    q_away = turn(tie(queries, q_far)[0], -1)
    part, h0, h1, h2, h3 = latent_part(
        scalars, keep, got, r1, r2, r3, input_norm_gain.reshape(1, -1), weight
    )
    cosine, sine = tables(scalars, tie(segment_ordering, part)[0])
    p1, p2, p3 = (shift(part, "zl", k) for k in (1, 2, 3))
    rows = kv_rows([part, p1, p2, p3], cosine, sine, latent_norm_gain.reshape(1, -1))
    rows, h1, h2, h3 = tie(rows, h1, h2, h3)
    beside = swap(rows, "zh")
    pieces = [h0] + [shift(h, "zl", k) for k, h in ((1, h1), (2, h2), (3, h3))]
    both = pack([rows, beside], (q_far, q_back, *pieces[1:]))
    column = [both] + [shift(both, "y", -k) for k in (1, 2, 3)]
    keys = column + [swap(value, "core") for value in column]

    *keys, q_away = tie(*keys, q_away)
    lifted = lift(scalars, segment_ordering, keys, latent_up_weight)
    relayed, direct = attend((far, back), scalars, segment_ordering, [q_far, q_back], lifted)
    got = turn(relayed, 1)
    mine, own = attend((away, near), scalars, segment_ordering, [q_away, queries], lifted)
    direct, own = tie(direct, own)
    direct = turn(direct, -1)
    passed = turn(relay(got, mine), 1)
    hidden = hidden_rows(scalars, pieces)
    return hidden, merge(own, direct, passed)


def solution(mesh):
    split = Mesh(mesh.devices.reshape(SIZES), AXES)
    ctx, tp = ("y", "x", "zh"), ("zl", "core")
    in_specs = (
        P(),
        P(ctx, tp),
        P(ctx + tp, None),
        P(ctx, tp),
        P(tp, None),
        P(tp, None),
        P(),
        P(),
        P(ctx, None),
        P(),
        P(None, tp),
    )
    out_specs = (P(ctx + tp, None), P(ctx, tp))
    return jax.shard_map(body, mesh=split, in_specs=in_specs, out_specs=out_specs, check_vma=False)
```

```python
import functools
import math

import jax
import jax.numpy as jnp
from jax import lax
from jax.experimental import pallas as pl
from jax.experimental.pallas import tpu as pltpu
from jax.sharding import Mesh, PartitionSpec as P

LATENT = 512
ROPE = 64
NOPE = 128
VDIM = 128
HEADS = 8
WIDE = 640
MESSAGE = HEADS * VDIM + 128
COLS = 896
BF = jnp.bfloat16
F32 = jnp.float32
MIB = 1 << 20
AXES = ("y", "x", "zh", "zl", "core")
SIZES = (4, 4, 2, 4, 2)
ORDER = (2, 1, 3, 0)


def dot(a, b):
    return jnp.dot(a, b, preferred_element_type=F32)


def shift(value, axis, k):
    return lax.ppermute(value, axis, [(i, (i + k) % 4) for i in range(4)])


def swap(value, axis, bit=1, size=2):
    return lax.ppermute(value, axis, [(i, i ^ bit) for i in range(size)])


def flat(y, x, zh, zl, core):
    return (((y * 4 + x) * 2 + zh) * 4 + zl) * 2 + core


def turn(value, k):
    perm = []
    for x in range(4):
        for core in range(2):
            perm.append((x * 2 + core, (x + (k if core == 0 else -k)) % 4 * 2 + core))
    return lax.ppermute(value, ("x", "core"), perm)


def tie(*values):
    return lax.optimization_barrier(values)


def near_block(value):
    same = ((1, 0), (1, 1), (2, 0), (2, 1))
    crossing = ((3, 0), (3, 1), (0, 0), (0, 1))
    perm = []
    for y in range(4):
        for x in range(4):
            for zh in range(2):
                for zl in range(4):
                    for core in range(2):
                        source = same[zl] if core == zh else crossing[zl]
                        perm.append((flat(y ^ zl, x, core, *source), flat(y, x, zh, zl, core)))
    return lax.ppermute(value, AXES, perm)


def cross(value):
    perm = [(zh * 4 + zl, (1 - zh) * 4 + (zl ^ 2)) for zh in range(2) for zl in range(4)]
    return lax.ppermute(value, ("zh", "zl"), perm)


def coords(s):
    f = s[0]
    return f // 64, f // 16 % 4, f // 8 % 2, f // 2 % 4, f % 2


def params(mib):
    return pltpu.CompilerParams(vmem_limit_bytes=int(mib * MIB))


def shape(dims, dtype=BF):
    return jax.ShapeDtypeStruct(dims, dtype)


def project_kernel(s, x_hbm, ad_hbm, w_hbm, au_hbm, res_hbm, send_ref, keep_ref, x, ad, w, au, res, xr, kept, sem):
    y, _, _, zl, core = coords(s)
    columns = [pl.ds(pl.multiple_of((y ^ ((zl + k) % 4)) * COLS, 128), COLS) for k in ORDER]

    def fetch(source, target, index):
        copy = pltpu.make_async_copy(source, target, sem.at[index])
        copy.start()
        return copy

    first = [fetch(x_hbm, x, 0), fetch(ad_hbm, ad, 1)]
    weights = [fetch(w_hbm.at[:, column], w.at[b], 4 + b) for b, column in enumerate(columns[:1])]
    second = [fetch(au_hbm, au, 2), fetch(res_hbm, res, 3)]
    weights += [fetch(w_hbm.at[:, column], w.at[b + 1], 5 + b) for b, column in enumerate(columns[1:])]
    for copy in first:
        copy.wait()
    xr[0:64, :] = x[:, 1 - core].reshape(64, 1024)
    xr[64:128, :] = x[:, core].reshape(64, 1024)
    down = dot(xr[...], ad[...])
    high = down.astype(BF)
    pieces = jnp.concatenate([high, (down - high.astype(F32)).astype(BF)], axis=0)
    rows = pl.ds(pl.multiple_of(zl * 16, 16), 16)
    for b, column in enumerate(columns):
        weights[b].wait()
        acc = dot(xr[...], w[b])
        if b == 0:
            for copy in second:
                copy.wait()
        adapter = dot(pieces, au[:, column])
        acc = acc + adapter[:128] + adapter[128:]
        send_ref[b] = acc[:64].astype(BF)
        kept[...] = acc[64:]
        kept[rows, :] = kept[rows, :] + res[:, column].astype(F32)
        keep_ref[b] = kept[...].astype(BF)


def project(scalars, *operands):
    return pl.pallas_call(
        project_kernel,
        in_specs=[pl.BlockSpec(memory_space=pltpu.SMEM)] + [pl.BlockSpec(memory_space=pltpu.HBM)] * 5,
        out_specs=[pl.BlockSpec(memory_space=pltpu.VMEM)] * 2,
        out_shape=[shape((4, 64, COLS))] * 2,
        scratch_shapes=[
            pltpu.VMEM((4, 2, 16, 1024), BF),
            pltpu.VMEM((1024, 256), BF),
            pltpu.VMEM((4, 1024, COLS), BF),
            pltpu.VMEM((256, 4 * COLS), BF),
            pltpu.VMEM((16, 4 * COLS), BF),
            pltpu.VMEM((128, 1024), BF),
            pltpu.VMEM((64, COLS), F32),
            pltpu.SemaphoreType.DMA((8,)),
        ],
        compiler_params=params(52.5),
        name="project",
    )(scalars, *operands)


def local(kernel, outs, mib, name, smem=0, vmem=0, scratch=()):
    space = lambda kind, n: [pl.BlockSpec(memory_space=kind)] * n
    out_specs = pl.BlockSpec(memory_space=pltpu.VMEM)
    return pl.pallas_call(
        kernel,
        in_specs=space(pltpu.SMEM, smem) + space(pltpu.VMEM, vmem),
        out_specs=[out_specs] * len(outs) if isinstance(outs, list) else out_specs,
        out_shape=outs,
        scratch_shapes=scratch,
        compiler_params=params(mib),
        name=name,
    )


def pair_sum_kernel(keep_ref, got_ref, *outs):
    for k, out in enumerate(outs):
        out[...] = (keep_ref[k].astype(F32) + got_ref[k].astype(F32)).astype(BF)


def pair_sum(keep, got, count):
    return local(pair_sum_kernel, [shape((64, COLS))] * count, 16, "pair_sum", vmem=2)(keep, got)


def pack_kernel(count, *refs):
    out_ref = refs[-1]
    start = 0
    for ref in refs[:count]:
        size = ref.shape[0]
        out_ref[start : start + size] = ref[...]
        start += size


def pack(blocks, after):
    dims = (sum(block.shape[0] for block in blocks),) + blocks[0].shape[1:]
    kernel = functools.partial(pack_kernel, len(blocks))
    return local(kernel, shape(dims), 16, "pack", vmem=len(blocks) + len(after))(*blocks, *after)


def assemble_kernel(s, own_ref, other_ref, out_ref):
    _, x, _, _, core = coords(s)
    out_ref[:, 512:] = jnp.zeros((COLS, WIDE - 512), BF)
    for k in range(4):
        for other, ref in enumerate((own_ref, other_ref)):
            zh = (core + other) % 2
            row = pl.multiple_of((x ^ k) * 224 + zh * 112, 16)
            out_ref[pl.ds(row, 112), 0:576] = ref[k]


def assemble(scalars, own, other):
    return local(assemble_kernel, shape((COLS, WIDE)), 16, "assemble", 1, 2)(scalars, own, other)


def tables_kernel(s, seg, cos_ref, sin_ref):
    y, x, zh, _, core = coords(s)
    ctx = y * 8 + x * 2 + zh
    row = lax.broadcasted_iota(jnp.int32, (64, ROPE), 0)
    lane = lax.broadcasted_iota(jnp.int32, (64, ROPE), 1)
    token = row // 16 * 32 + core * 16 + row % 16
    places = jnp.where(token < 64, seg[2 * ctx], seg[2 * ctx + 1]) * 64 + token % 64
    inverse = jnp.exp((lane % 32).astype(F32) * (-2.0 * math.log(10000.0) / ROPE))
    angles = places.astype(F32) * inverse
    cos_ref[...] = jnp.cos(angles)
    sine = jnp.sin(angles)
    sin_ref[...] = jnp.where(lane < 32, -sine, sine)


def tables(scalars, seg):
    return local(tables_kernel, [shape((64, ROPE), F32)] * 2, 16, "tables", 2)(scalars, seg)


def latent_kernel(s, keep_ref, got_ref, r1, r2, r3, gain_ref, w_ref, part_ref, h0, h1, h2, h3, hid):
    y, _, _, zl, _ = coords(s)
    total = sum(ref[...].astype(F32) for ref in (keep_ref.at[3], got_ref.at[3], r1, r2, r3))
    hidden = total.astype(BF)
    hid[...] = hidden
    for k, out in enumerate((h0, h1, h2, h3)):
        out[...] = hid[pl.ds(pl.multiple_of(((zl + k) % 4) * 16, 16), 16), :]
    wide = hidden.astype(F32)
    squares = jnp.sum(wide * wide, axis=1, keepdims=True)
    gain = gain_ref[:, pl.ds(pl.multiple_of((y ^ zl) * COLS, 128), COLS)].astype(F32)
    part = dot((wide * gain).astype(BF), w_ref[...])
    lane = lax.broadcasted_iota(jnp.int32, (64, 128), 1)
    high = squares.astype(BF).astype(F32)
    tail = jnp.where(lane == 64, high, jnp.where(lane == 65, squares - high, part[:, 512:]))
    part_ref[:, :512] = part[:, :512].astype(BF)
    part_ref[:, 512:] = tail.astype(BF)


def latent_part(scalars, *operands):
    outs = [shape((64, WIDE))] + [shape((16, COLS))] * 4
    scratch = [pltpu.VMEM((64, COLS), BF)]
    return local(latent_kernel, outs, 16, "latent_part", 1, 7, scratch)(scalars, *operands)


def rows_kernel(p0, p1, p2, p3, cos_ref, sin_ref, gain_ref, out_ref):
    total = p0[...].astype(F32) + p1[...].astype(F32) + p2[...].astype(F32) + p3[...].astype(F32)
    tail = total[:, 512:]
    inverse = lax.rsqrt((tail[:, 64:65] + tail[:, 65:66]) / 3584.0 + 1e-06)
    latent = total[:, :512] * inverse
    mean_square = jnp.mean(latent * latent, axis=1, keepdims=True)
    out_ref[:, :512] = (latent * lax.rsqrt(mean_square + 1e-06) * gain_ref[...].astype(F32)).astype(BF)
    rope = tail[:, :64] * inverse
    swapped = jnp.concatenate([rope[:, 32:], rope[:, :32]], axis=1)
    rotated = rope * cos_ref[...] + swapped * sin_ref[...]
    out_ref[:, 512:] = jnp.concatenate([rotated, jnp.zeros((64, 64), F32)], axis=1).astype(BF)


def kv_rows(parts, cosine, sine, gain):
    return local(rows_kernel, shape((64, WIDE)), 16, "kv_rows", vmem=7)(*parts, cosine, sine, gain)


def lift_kernel(s, seg, *refs):
    keys = refs[:8]
    up_ref, key_ref, value_ref, kv = refs[8:]
    y, x, zh, _, _ = coords(s)
    for k in range(4):
        for a in range(2):
            ctx = ((y + k) % 4) * 8 + x * 2 + (zh + a) % 2
            first_upper = (seg[2 * ctx] > seg[2 * ctx + 1]).astype(jnp.int32)
            for half in range(2):
                upper = first_upper if half == 0 else 1 - first_upper
                for other in range(2):
                    row = pl.multiple_of(upper * 512 + (k * 2 + a) * 64 + other * 32, 32)
                    start = a * 64 + half * 32
                    kv[pl.ds(row, 32), :] = keys[4 * other + k][start : start + 32, :]
    ones = jnp.ones((1024, 128), BF)
    for head in range(HEADS):
        lifted = dot(kv[:, :LATENT], up_ref[:, head * 256 : head * 256 + 256]).astype(BF)
        key_ref[head, :, :NOPE] = lifted[:, :NOPE]
        key_ref[head, :, NOPE:] = kv[:, LATENT:]
        value_ref[head, :, :VDIM] = lifted[:, NOPE:]
        value_ref[head, :, VDIM:] = ones


def lift(scalars, seg, keys, up):
    outs = [shape((HEADS, 1024, 256))] * 2
    scratch = [pltpu.VMEM((1024, WIDE), BF)]
    return local(lift_kernel, outs, 24, "lift", 2, 9, scratch)(scalars, seg, *keys, up)


def stat_pieces(level, lane):
    high = level.astype(BF).astype(F32)
    middle = (level - high).astype(BF).astype(F32)
    return jnp.where(lane < 8, high, jnp.where(lane < 16, middle, level - high - middle))


def attend_kernel(chunks, s, seg, *refs):
    count = len(chunks)
    queries = refs[:count]
    key_ref, value_ref = refs[count : count + 2]
    outs = refs[count + 2 :]
    y, x, zh, _, core = coords(s)
    hops = (0, 1 + 2 * core, 2, 3 - 2 * core)
    factor = math.log2(math.e) / math.sqrt(NOPE + ROPE)
    lane = lax.broadcasted_iota(jnp.int32, (1, 512), 1)
    lower = jnp.zeros((1, 512), jnp.int32)
    upper = lower
    for k in range(4):
        for a in range(2):
            ctx = ((y + k) % 4) * 8 + x * 2 + (zh + a) % 2
            one, two = seg[2 * ctx], seg[2 * ctx + 1]
            lower = jnp.where(lane // 64 == k * 2 + a, jnp.minimum(one, two), lower)
            upper = jnp.where(lane // 64 == k * 2 + a, jnp.maximum(one, two), upper)
    inside = (lane // 16) % 2 * 32 + ((lane // 32) % 2 + core) % 2 * 16 + lane % 16
    row = lax.broadcasted_iota(jnp.int32, (64, 512), 0)
    low_rows, high_rows, low_bias, high_bias = [], [], [], []
    for chunk in chunks:
        ctx = y * 8 + ((x + hops[chunk]) % 4) * 2 + zh
        one, two = seg[2 * ctx], seg[2 * ctx + 1]
        flipped = (one > two).astype(jnp.int32)
        low_rows.append(pl.ds(pl.multiple_of(flipped * 64, 64), 64))
        high_rows.append(pl.ds(pl.multiple_of(64 - flipped * 64, 64), 64))
        low_bias.append(jnp.where(lower * 64 + inside <= row + jnp.minimum(one, two) * 64, 0.0, -1e30))
        high_bias.append(jnp.where(upper * 64 + inside <= row + jnp.maximum(one, two) * 64, 0.0, -1e30))
    low_bias = jnp.concatenate(low_bias, axis=0)
    high_bias = jnp.concatenate(high_bias, axis=0)
    rows = 64 * count
    stat_lane = lax.broadcasted_iota(jnp.int32, (2 * rows, 128), 1)
    stats = jnp.zeros((2 * rows, 128), F32)
    across = (((1,), (1,)), ((), ()))
    near, far = [], []
    for head in range(HEADS):
        column = slice(head * 192, head * 192 + 192)
        pieces = [q[r, column] for q, r in zip(queries, low_rows)] + [q[r, column] for q, r in zip(queries, high_rows)]
        query = jnp.concatenate([jnp.concatenate(pieces, axis=0), jnp.zeros((2 * rows, 64), BF)], axis=1)
        near.append(lax.dot_general(query, key_ref[head, :512, :], across, preferred_element_type=F32))
        high = lax.dot_general(query[rows:], key_ref[head, 512:, :], across, preferred_element_type=F32)
        far.append(high + high_bias)
    low = [scores[:rows] + low_bias for scores in near]
    mid = [scores[rows:] for scores in near]
    low_top = [jnp.max(scores, axis=1, keepdims=True) for scores in low]
    high_top = [jnp.max(jnp.maximum(a, b), axis=1, keepdims=True) for a, b in zip(mid, far)]
    weigh = lambda scores, top: jnp.exp2((scores - top) * factor).astype(BF)
    low = [weigh(a, t) for a, t in zip(low, low_top)]
    mid = [weigh(a, t) for a, t in zip(mid, high_top)]
    far = [weigh(a, t) for a, t in zip(far, high_top)]
    first = [dot(jnp.concatenate([a, b], axis=0), value_ref[h, :512, :]) for h, (a, b) in enumerate(zip(low, mid))]
    second = [dot(a, value_ref[h, 512:, :]) for h, a in enumerate(far)]
    for head in range(HEADS):
        both = jnp.concatenate([first[head][:rows], first[head][rows:] + second[head]], axis=0)
        top = jnp.concatenate([low_top[head], high_top[head]], axis=0)
        mixed = (both[:, :VDIM] / both[:, VDIM:]).astype(BF)
        level = top * factor + jnp.log2(both[:, VDIM:])
        stats = jnp.where(stat_lane % 8 == head, level, stats)
        for c in range(count):
            column = slice(head * 128, head * 128 + 128)
            outs[c][low_rows[c], column] = mixed[64 * c : 64 * c + 64]
            outs[c][high_rows[c], column] = mixed[rows + 64 * c : rows + 64 * c + 64]
    stats = jnp.where(stat_lane < 24, stat_pieces(stats, stat_lane), 0.0).astype(BF)
    for c in range(count):
        outs[c][low_rows[c], HEADS * 128 :] = stats[64 * c : 64 * c + 64]
        outs[c][high_rows[c], HEADS * 128 :] = stats[rows + 64 * c : rows + 64 * c + 64]


def attend(chunks, scalars, seg, queries, lifted):
    kernel = functools.partial(attend_kernel, chunks)
    outs = [shape((128, MESSAGE))] * len(chunks)
    return local(kernel, outs, 32, "attend", 2, len(chunks) + 2)(scalars, seg, *queries, *lifted)


def spread_levels(ref, width, group):
    row = lax.broadcasted_iota(jnp.int32, (128, width), 0)
    lane = lax.broadcasted_iota(jnp.int32, (128, width), 1)
    picks = (row < 24) & (row % 8 == (lane // group) % 8)
    return dot(ref[:, HEADS * 128 :], picks.astype(F32).astype(BF))


def merged(refs):
    levels = [spread_levels(ref, 1024, 128) for ref in refs]
    top = functools.reduce(jnp.maximum, levels)
    scales = [jnp.exp2(level - top) for level in levels]
    mixed = sum(ref[:, : HEADS * 128].astype(F32) * scale for ref, scale in zip(refs, scales))
    return (mixed / sum(scales[1:], scales[0])).astype(BF)


def relay_kernel(got_ref, own_ref, out_ref):
    refs = (got_ref, own_ref)
    out_ref[:, : HEADS * 128] = merged(refs)
    one, two = [spread_levels(ref, 128, 1) for ref in refs]
    top = jnp.maximum(one, two)
    level = top + jnp.log2(jnp.exp2(one - top) + jnp.exp2(two - top))
    lane = lax.broadcasted_iota(jnp.int32, (128, 128), 1)
    out_ref[:, HEADS * 128 :] = jnp.where(lane < 24, stat_pieces(level, lane), 0.0).astype(BF)


def relay(got, own):
    return local(relay_kernel, shape((128, MESSAGE)), 16, "relay", vmem=2)(got, own)


def merge_kernel(a_ref, b_ref, c_ref, out_ref):
    out_ref[...] = merged((a_ref, b_ref, c_ref))


def merge(a, b, c):
    return local(merge_kernel, shape((128, HEADS * VDIM)), 16, "merge", vmem=3)(a, b, c)


def hidden_kernel(s, h0, h1, h2, h3, out_ref):
    y, _, _, zl, _ = coords(s)
    for k, ref in enumerate((h0, h1, h2, h3)):
        column = pl.multiple_of((y ^ ((zl + 4 - k) % 4)) * COLS, 128)
        out_ref[:, pl.ds(column, COLS)] = ref[...]


def hidden_rows(scalars, blocks):
    return local(hidden_kernel, shape((16, 4 * COLS)), 16, "hidden_rows", 1, 4)(scalars, *blocks)


def body(
    segment_ordering,
    attention_input,
    residual,
    queries,
    output_weight,
    adapter_down_factor,
    adapter_up_factor,
    input_norm_gain,
    latent_key_weight,
    latent_norm_gain,
    latent_up_weight,
):
    scalars = lax.axis_index(AXES).astype(jnp.int32).reshape(1)
    near, away, far, back = 0, 1, 2, 3

    block = near_block(latent_key_weight)[None]
    send, keep = project(
        scalars,
        attention_input.reshape(4, 2, 16, 1024),
        adapter_down_factor,
        output_weight,
        adapter_up_factor,
        residual,
    )
    block, send = tie(block, send)
    got = swap(send, "core")
    blocks = [block] + [swap(block, "x", k, 4) for k in (1, 2, 3)]
    sums = pair_sum(keep, got, 3)
    r2, r1, r3 = (shift(value, "zl", k) for value, k in zip(sums, ORDER))
    four = pack(blocks, (r1, r2, r3))
    weight = assemble(scalars, four, swap(four, "core"))
    q_far, q_back = shift(queries, "x", 2), turn(queries, 1)
    q_away = turn(tie(queries, q_far)[0], -1)
    part, h0, h1, h2, h3 = latent_part(
        scalars, keep, got, r1, r2, r3, input_norm_gain.reshape(1, -1), weight
    )
    cosine, sine = tables(scalars, tie(segment_ordering, part)[0])
    p1, p2, p3 = (shift(part, "zl", k) for k in (1, 2, 3))
    rows = kv_rows([part, p1, p2, p3], cosine, sine, latent_norm_gain.reshape(1, -1))
    rows, h1, h2, h3 = tie(rows, h1, h2, h3)
    beside = cross(rows)
    pieces = [h0] + [shift(h, "zl", k) for k, h in ((1, h1), (2, h2), (3, h3))]
    both = pack([rows, beside], (q_far, q_back, *pieces[1:]))
    column = [both] + [shift(both, "y", -k) for k in (1, 2, 3)]
    keys = column + [swap(value, "core") for value in column]

    *keys, q_away = tie(*keys, q_away)
    lifted = lift(scalars, segment_ordering, keys, latent_up_weight)
    (relayed,) = attend((far,), scalars, segment_ordering, [q_far], lifted)
    got = turn(relayed, 1)
    direct, mine = attend((back, away), scalars, segment_ordering, [q_back, q_away], lifted)
    direct = turn(direct, -1)
    passed = turn(relay(got, mine), 1)
    (own,) = attend((near,), scalars, segment_ordering, [queries], lifted)
    hidden = hidden_rows(scalars, pieces)
    return hidden, merge(own, direct, passed)


def solution(mesh):
    split = Mesh(mesh.devices.reshape(SIZES), AXES)
    ctx, tp = ("y", "x", "zh"), ("zl", "core")
    in_specs = (
        P(),
        P(ctx, tp),
        P(ctx + tp, None),
        P(ctx, tp),
        P(tp, None),
        P(tp, None),
        P(),
        P(),
        P(ctx, None),
        P(),
        P(None, tp),
    )
    out_specs = (P(ctx + tp, None), P(ctx, tp))
    return jax.shard_map(body, mesh=split, in_specs=in_specs, out_specs=out_specs, check_vma=False)
```

```python
import functools
import math

import jax
import jax.numpy as jnp
from jax import lax
from jax.experimental import pallas as pl
from jax.experimental.pallas import tpu as pltpu
from jax.sharding import Mesh, PartitionSpec as P

LATENT = 512
ROPE = 64
NOPE = 128
VDIM = 128
HEADS = 8
WIDE = 640
MESSAGE = HEADS * VDIM + 128
COLS = 896
BF = jnp.bfloat16
F32 = jnp.float32
MIB = 1 << 20
AXES = ("y", "x", "zh", "zl", "core")
SIZES = (4, 4, 2, 4, 2)
ORDER = (2, 1, 3, 0)


def dot(a, b):
    return jnp.dot(a, b, preferred_element_type=F32)


def shift(value, axis, k):
    return lax.ppermute(value, axis, [(i, (i + k) % 4) for i in range(4)])


def swap(value, axis, bit=1, size=2):
    return lax.ppermute(value, axis, [(i, i ^ bit) for i in range(size)])


def flat(y, x, zh, zl, core):
    return (((y * 4 + x) * 2 + zh) * 4 + zl) * 2 + core


def turn(value, k):
    perm = []
    for x in range(4):
        for core in range(2):
            perm.append((x * 2 + core, (x + (k if core == 0 else -k)) % 4 * 2 + core))
    return lax.ppermute(value, ("x", "core"), perm)


def tie(*values):
    return lax.optimization_barrier(values)


def near_block(value):
    same = ((1, 0), (1, 1), (2, 0), (2, 1))
    crossing = ((3, 0), (3, 1), (0, 0), (0, 1))
    perm = []
    for y in range(4):
        for x in range(4):
            for zh in range(2):
                for zl in range(4):
                    for core in range(2):
                        source = same[zl] if core == zh else crossing[zl]
                        perm.append((flat(y ^ zl, x, core, *source), flat(y, x, zh, zl, core)))
    return lax.ppermute(value, AXES, perm)


def cross(value):
    perm = [(zh * 4 + zl, (1 - zh) * 4 + (zl ^ 2)) for zh in range(2) for zl in range(4)]
    return lax.ppermute(value, ("zh", "zl"), perm)


def coords(s):
    f = s[0]
    return f // 64, f // 16 % 4, f // 8 % 2, f // 2 % 4, f % 2


def params(mib):
    return pltpu.CompilerParams(vmem_limit_bytes=int(mib * MIB))


def shape(dims, dtype=BF):
    return jax.ShapeDtypeStruct(dims, dtype)


def project_kernel(s, x_hbm, ad_hbm, w_hbm, au_hbm, res_hbm, send_ref, keep_ref, x, ad, w, au, res, xr, kept, sem):
    y, _, _, zl, core = coords(s)
    columns = [pl.ds(pl.multiple_of((y ^ ((zl + k) % 4)) * COLS, 128), COLS) for k in ORDER]

    def fetch(source, target, index):
        copy = pltpu.make_async_copy(source, target, sem.at[index])
        copy.start()
        return copy

    first = [fetch(x_hbm, x, 0), fetch(ad_hbm, ad, 1)]
    weights = [fetch(w_hbm.at[:, column], w.at[b], 4 + b) for b, column in enumerate(columns[:1])]
    second = [fetch(au_hbm, au, 2), fetch(res_hbm, res, 3)]
    weights += [fetch(w_hbm.at[:, column], w.at[b + 1], 5 + b) for b, column in enumerate(columns[1:])]
    for copy in first:
        copy.wait()
    xr[0:64, :] = x[:, 1 - core].reshape(64, 1024)
    xr[64:128, :] = x[:, core].reshape(64, 1024)
    down = dot(xr[...], ad[...])
    high = down.astype(BF)
    pieces = jnp.concatenate([high, (down - high.astype(F32)).astype(BF)], axis=0)
    rows = pl.ds(pl.multiple_of(zl * 16, 16), 16)
    for b, column in enumerate(columns):
        weights[b].wait()
        acc = dot(xr[...], w[b])
        if b == 0:
            for copy in second:
                copy.wait()
        adapter = dot(pieces, au[:, column])
        acc = acc + adapter[:128] + adapter[128:]
        send_ref[b] = acc[:64].astype(BF)
        kept[...] = acc[64:]
        kept[rows, :] = kept[rows, :] + res[:, column].astype(F32)
        keep_ref[b] = kept[...].astype(BF)


def project(scalars, *operands):
    return pl.pallas_call(
        project_kernel,
        in_specs=[pl.BlockSpec(memory_space=pltpu.SMEM)] + [pl.BlockSpec(memory_space=pltpu.HBM)] * 5,
        out_specs=[pl.BlockSpec(memory_space=pltpu.VMEM)] * 2,
        out_shape=[shape((4, 64, COLS))] * 2,
        scratch_shapes=[
            pltpu.VMEM((4, 2, 16, 1024), BF),
            pltpu.VMEM((1024, 256), BF),
            pltpu.VMEM((4, 1024, COLS), BF),
            pltpu.VMEM((256, 4 * COLS), BF),
            pltpu.VMEM((16, 4 * COLS), BF),
            pltpu.VMEM((128, 1024), BF),
            pltpu.VMEM((64, COLS), F32),
            pltpu.SemaphoreType.DMA((8,)),
        ],
        compiler_params=params(52.5),
        name="project",
    )(scalars, *operands)


def local(kernel, outs, mib, name, smem=0, vmem=0, scratch=()):
    space = lambda kind, n: [pl.BlockSpec(memory_space=kind)] * n
    out_specs = pl.BlockSpec(memory_space=pltpu.VMEM)
    return pl.pallas_call(
        kernel,
        in_specs=space(pltpu.SMEM, smem) + space(pltpu.VMEM, vmem),
        out_specs=[out_specs] * len(outs) if isinstance(outs, list) else out_specs,
        out_shape=outs,
        scratch_shapes=scratch,
        compiler_params=params(mib),
        name=name,
    )


def pair_sum_kernel(keep_ref, got_ref, *outs):
    for k, out in enumerate(outs):
        out[...] = (keep_ref[k].astype(F32) + got_ref[k].astype(F32)).astype(BF)


def pair_sum(keep, got, count):
    return local(pair_sum_kernel, [shape((64, COLS))] * count, 16, "pair_sum", vmem=2)(keep, got)


def pack_kernel(count, *refs):
    out_ref = refs[-1]
    start = 0
    for ref in refs[:count]:
        size = ref.shape[0]
        out_ref[start : start + size] = ref[...]
        start += size


def pack(blocks, after):
    dims = (sum(block.shape[0] for block in blocks),) + blocks[0].shape[1:]
    kernel = functools.partial(pack_kernel, len(blocks))
    return local(kernel, shape(dims), 16, "pack", vmem=len(blocks) + len(after))(*blocks, *after)


def assemble_kernel(s, own_ref, other_ref, out_ref):
    _, x, _, _, core = coords(s)
    out_ref[:, 512:] = jnp.zeros((COLS, WIDE - 512), BF)
    for k in range(4):
        for other, ref in enumerate((own_ref, other_ref)):
            zh = (core + other) % 2
            row = pl.multiple_of((x ^ k) * 224 + zh * 112, 16)
            out_ref[pl.ds(row, 112), 0:576] = ref[k]


def assemble(scalars, own, other):
    return local(assemble_kernel, shape((COLS, WIDE)), 16, "assemble", 1, 2)(scalars, own, other)


def tables_kernel(s, seg, cos_ref, sin_ref):
    y, x, zh, _, core = coords(s)
    ctx = y * 8 + x * 2 + zh
    row = lax.broadcasted_iota(jnp.int32, (64, ROPE), 0)
    lane = lax.broadcasted_iota(jnp.int32, (64, ROPE), 1)
    token = row // 16 * 32 + core * 16 + row % 16
    places = jnp.where(token < 64, seg[2 * ctx], seg[2 * ctx + 1]) * 64 + token % 64
    inverse = jnp.exp((lane % 32).astype(F32) * (-2.0 * math.log(10000.0) / ROPE))
    angles = places.astype(F32) * inverse
    cos_ref[...] = jnp.cos(angles)
    sine = jnp.sin(angles)
    sin_ref[...] = jnp.where(lane < 32, -sine, sine)


def tables(scalars, seg):
    return local(tables_kernel, [shape((64, ROPE), F32)] * 2, 16, "tables", 2)(scalars, seg)


def latent_kernel(s, keep_ref, got_ref, r1, r2, r3, gain_ref, w_ref, part_ref, h0, h1, h2, h3, hid):
    y, _, _, zl, _ = coords(s)
    total = sum(ref[...].astype(F32) for ref in (keep_ref.at[3], got_ref.at[3], r1, r2, r3))
    hidden = total.astype(BF)
    hid[...] = hidden
    for k, out in enumerate((h0, h1, h2, h3)):
        out[...] = hid[pl.ds(pl.multiple_of(((zl + k) % 4) * 16, 16), 16), :]
    wide = hidden.astype(F32)
    squares = jnp.sum(wide * wide, axis=1, keepdims=True)
    gain = gain_ref[:, pl.ds(pl.multiple_of((y ^ zl) * COLS, 128), COLS)].astype(F32)
    part = dot((wide * gain).astype(BF), w_ref[...])
    lane = lax.broadcasted_iota(jnp.int32, (64, 128), 1)
    high = squares.astype(BF).astype(F32)
    tail = jnp.where(lane == 64, high, jnp.where(lane == 65, squares - high, part[:, 512:]))
    part_ref[:, :512] = part[:, :512].astype(BF)
    part_ref[:, 512:] = tail.astype(BF)


def latent_part(scalars, *operands):
    outs = [shape((64, WIDE))] + [shape((16, COLS))] * 4
    scratch = [pltpu.VMEM((64, COLS), BF)]
    return local(latent_kernel, outs, 16, "latent_part", 1, 7, scratch)(scalars, *operands)


def rows_kernel(p0, p1, p2, p3, cos_ref, sin_ref, gain_ref, out_ref):
    total = p0[...].astype(F32) + p1[...].astype(F32) + p2[...].astype(F32) + p3[...].astype(F32)
    tail = total[:, 512:]
    inverse = lax.rsqrt((tail[:, 64:65] + tail[:, 65:66]) / 3584.0 + 1e-06)
    latent = total[:, :512] * inverse
    mean_square = jnp.mean(latent * latent, axis=1, keepdims=True)
    out_ref[:, :512] = (latent * lax.rsqrt(mean_square + 1e-06) * gain_ref[...].astype(F32)).astype(BF)
    rope = tail[:, :64] * inverse
    swapped = jnp.concatenate([rope[:, 32:], rope[:, :32]], axis=1)
    rotated = rope * cos_ref[...] + swapped * sin_ref[...]
    out_ref[:, 512:] = jnp.concatenate([rotated, jnp.zeros((64, 64), F32)], axis=1).astype(BF)


def kv_rows(parts, cosine, sine, gain):
    return local(rows_kernel, shape((64, WIDE)), 16, "kv_rows", vmem=7)(*parts, cosine, sine, gain)


def lift_kernel(s, seg, *refs):
    keys = refs[:8]
    up_ref, key_ref, value_ref, kv = refs[8:]
    y, x, zh, _, _ = coords(s)
    for k in range(4):
        for a in range(2):
            ctx = ((y + k) % 4) * 8 + x * 2 + (zh + a) % 2
            first_upper = (seg[2 * ctx] > seg[2 * ctx + 1]).astype(jnp.int32)
            for half in range(2):
                upper = first_upper if half == 0 else 1 - first_upper
                for other in range(2):
                    row = pl.multiple_of(upper * 512 + (k * 2 + a) * 64 + other * 32, 32)
                    start = a * 64 + half * 32
                    kv[pl.ds(row, 32), :] = keys[4 * other + k][start : start + 32, :]
    ones = jnp.ones((1024, 128), BF)
    for head in range(HEADS):
        lifted = dot(kv[:, :LATENT], up_ref[:, head * 256 : head * 256 + 256]).astype(BF)
        key_ref[head, :, :NOPE] = lifted[:, :NOPE]
        key_ref[head, :, NOPE:] = kv[:, LATENT:]
        value_ref[head, :, :VDIM] = lifted[:, NOPE:]
        value_ref[head, :, VDIM:] = ones


def lift(scalars, seg, keys, up):
    outs = [shape((HEADS, 1024, 256))] * 2
    scratch = [pltpu.VMEM((1024, WIDE), BF)]
    return local(lift_kernel, outs, 24, "lift", 2, 9, scratch)(scalars, seg, *keys, up)


def stat_pieces(level, lane):
    high = level.astype(BF).astype(F32)
    middle = (level - high).astype(BF).astype(F32)
    return jnp.where(lane < 8, high, jnp.where(lane < 16, middle, level - high - middle))


def attend_kernel(chunks, s, seg, *refs):
    count = len(chunks)
    queries = refs[:count]
    key_ref, value_ref = refs[count : count + 2]
    outs = refs[count + 2 :]
    y, x, zh, _, core = coords(s)
    hops = (0, 1 + 2 * core, 2, 3 - 2 * core)
    factor = math.log2(math.e) / math.sqrt(NOPE + ROPE)
    lane = lax.broadcasted_iota(jnp.int32, (1, 512), 1)
    lower = jnp.zeros((1, 512), jnp.int32)
    upper = lower
    for k in range(4):
        for a in range(2):
            ctx = ((y + k) % 4) * 8 + x * 2 + (zh + a) % 2
            one, two = seg[2 * ctx], seg[2 * ctx + 1]
            lower = jnp.where(lane // 64 == k * 2 + a, jnp.minimum(one, two), lower)
            upper = jnp.where(lane // 64 == k * 2 + a, jnp.maximum(one, two), upper)
    inside = (lane // 16) % 2 * 32 + ((lane // 32) % 2 + core) % 2 * 16 + lane % 16
    row = lax.broadcasted_iota(jnp.int32, (64, 512), 0)
    low_rows, high_rows, low_bias, high_bias = [], [], [], []
    for chunk in chunks:
        ctx = y * 8 + ((x + hops[chunk]) % 4) * 2 + zh
        one, two = seg[2 * ctx], seg[2 * ctx + 1]
        flipped = (one > two).astype(jnp.int32)
        low_rows.append(pl.ds(pl.multiple_of(flipped * 64, 64), 64))
        high_rows.append(pl.ds(pl.multiple_of(64 - flipped * 64, 64), 64))
        low_bias.append(jnp.where(lower * 64 + inside <= row + jnp.minimum(one, two) * 64, 0.0, -1e30))
        high_bias.append(jnp.where(upper * 64 + inside <= row + jnp.maximum(one, two) * 64, 0.0, -1e30))
    low_bias = jnp.concatenate(low_bias, axis=0)
    high_bias = jnp.concatenate(high_bias, axis=0)
    rows = 64 * count
    stat_lane = lax.broadcasted_iota(jnp.int32, (2 * rows, 128), 1)
    stats = jnp.zeros((2 * rows, 128), F32)
    across = (((1,), (1,)), ((), ()))
    near, far = [], []
    for head in range(HEADS):
        column = slice(head * 192, head * 192 + 192)
        pieces = [q[r, column] for q, r in zip(queries, low_rows)] + [q[r, column] for q, r in zip(queries, high_rows)]
        query = jnp.concatenate([jnp.concatenate(pieces, axis=0), jnp.zeros((2 * rows, 64), BF)], axis=1)
        near.append(lax.dot_general(query, key_ref[head, :512, :], across, preferred_element_type=F32))
        high = lax.dot_general(query[rows:], key_ref[head, 512:, :], across, preferred_element_type=F32)
        far.append(high + high_bias)
    low = [scores[:rows] + low_bias for scores in near]
    mid = [scores[rows:] for scores in near]
    low_top = [jnp.max(scores, axis=1, keepdims=True) for scores in low]
    high_top = [jnp.max(jnp.maximum(a, b), axis=1, keepdims=True) for a, b in zip(mid, far)]
    weigh = lambda scores, top: jnp.exp2((scores - top) * factor).astype(BF)
    low = [weigh(a, t) for a, t in zip(low, low_top)]
    mid = [weigh(a, t) for a, t in zip(mid, high_top)]
    far = [weigh(a, t) for a, t in zip(far, high_top)]
    first = [dot(jnp.concatenate([a, b], axis=0), value_ref[h, :512, :]) for h, (a, b) in enumerate(zip(low, mid))]
    second = [dot(a, value_ref[h, 512:, :]) for h, a in enumerate(far)]
    for head in range(HEADS):
        both = jnp.concatenate([first[head][:rows], first[head][rows:] + second[head]], axis=0)
        top = jnp.concatenate([low_top[head], high_top[head]], axis=0)
        mixed = (both[:, :VDIM] / both[:, VDIM:]).astype(BF)
        level = top * factor + jnp.log2(both[:, VDIM:])
        stats = jnp.where(stat_lane % 8 == head, level, stats)
        for c in range(count):
            column = slice(head * 128, head * 128 + 128)
            outs[c][low_rows[c], column] = mixed[64 * c : 64 * c + 64]
            outs[c][high_rows[c], column] = mixed[rows + 64 * c : rows + 64 * c + 64]
    stats = jnp.where(stat_lane < 24, stat_pieces(stats, stat_lane), 0.0).astype(BF)
    for c in range(count):
        outs[c][low_rows[c], HEADS * 128 :] = stats[64 * c : 64 * c + 64]
        outs[c][high_rows[c], HEADS * 128 :] = stats[rows + 64 * c : rows + 64 * c + 64]


def attend(chunks, scalars, seg, queries, lifted):
    kernel = functools.partial(attend_kernel, chunks)
    outs = [shape((128, MESSAGE))] * len(chunks)
    return local(kernel, outs, 32, "attend", 2, len(chunks) + 2)(scalars, seg, *queries, *lifted)


def spread_levels(ref, width, group):
    row = lax.broadcasted_iota(jnp.int32, (128, width), 0)
    lane = lax.broadcasted_iota(jnp.int32, (128, width), 1)
    picks = (row < 24) & (row % 8 == (lane // group) % 8)
    return dot(ref[:, HEADS * 128 :], picks.astype(F32).astype(BF))


def merged(refs):
    levels = [spread_levels(ref, 1024, 128) for ref in refs]
    top = functools.reduce(jnp.maximum, levels)
    scales = [jnp.exp2(level - top) for level in levels]
    mixed = sum(ref[:, : HEADS * 128].astype(F32) * scale for ref, scale in zip(refs, scales))
    return (mixed / sum(scales[1:], scales[0])).astype(BF)


def relay_kernel(got_ref, own_ref, out_ref):
    refs = (got_ref, own_ref)
    out_ref[:, : HEADS * 128] = merged(refs)
    one, two = [spread_levels(ref, 128, 1) for ref in refs]
    top = jnp.maximum(one, two)
    level = top + jnp.log2(jnp.exp2(one - top) + jnp.exp2(two - top))
    lane = lax.broadcasted_iota(jnp.int32, (128, 128), 1)
    out_ref[:, HEADS * 128 :] = jnp.where(lane < 24, stat_pieces(level, lane), 0.0).astype(BF)


def relay(got, own):
    return local(relay_kernel, shape((128, MESSAGE)), 16, "relay", vmem=2)(got, own)


def final_kernel(s, a_ref, b_ref, c_ref, h0, h1, h2, h3, hidden_ref, attn_ref):
    y, _, _, zl, _ = coords(s)
    for k, ref in enumerate((h0, h1, h2, h3)):
        column = pl.multiple_of((y ^ ((zl + 4 - k) % 4)) * COLS, 128)
        hidden_ref[:, pl.ds(column, COLS)] = ref[...]
    attn_ref[...] = merged((a_ref, b_ref, c_ref))


def final(scalars, *operands):
    outs = [shape((16, 4 * COLS)), shape((128, HEADS * VDIM))]
    return local(final_kernel, outs, 16, "final", 1, 7)(scalars, *operands)


def body(
    segment_ordering,
    attention_input,
    residual,
    queries,
    output_weight,
    adapter_down_factor,
    adapter_up_factor,
    input_norm_gain,
    latent_key_weight,
    latent_norm_gain,
    latent_up_weight,
):
    scalars = lax.axis_index(AXES).astype(jnp.int32).reshape(1)
    near, away, far, back = 0, 1, 2, 3

    block = near_block(latent_key_weight)[None]
    send, keep = project(
        scalars,
        attention_input.reshape(4, 2, 16, 1024),
        adapter_down_factor,
        output_weight,
        adapter_up_factor,
        residual,
    )
    block, send = tie(block, send)
    got = swap(send, "core")
    blocks = [block] + [swap(block, "x", k, 4) for k in (1, 2, 3)]
    sums = pair_sum(keep, got, 3)
    r2, r1, r3 = (shift(value, "zl", k) for value, k in zip(sums, ORDER))
    four = pack(blocks, (r1, r2, r3))
    weight = assemble(scalars, four, swap(four, "core"))
    q_far, q_back = shift(queries, "x", 2), turn(queries, 1)
    q_away = turn(tie(queries, q_far)[0], -1)
    part, h0, h1, h2, h3 = latent_part(
        scalars, keep, got, r1, r2, r3, input_norm_gain.reshape(1, -1), weight
    )
    cosine, sine = tables(scalars, tie(segment_ordering, part)[0])
    p1, p2, p3 = (shift(part, "zl", k) for k in (1, 2, 3))
    rows = kv_rows([part, p1, p2, p3], cosine, sine, latent_norm_gain.reshape(1, -1))
    rows, h1, h2, h3 = tie(rows, h1, h2, h3)
    beside = cross(rows)
    pieces = [h0] + [shift(h, "zl", k) for k, h in ((1, h1), (2, h2), (3, h3))]
    both = pack([rows, beside], (q_far,))
    column = [both] + [shift(both, "y", -k) for k in (1, 2, 3)]
    keys = column + [swap(value, "core") for value in column]

    *keys, q_back, q_away = tie(*keys, q_back, q_away)
    lifted = lift(scalars, segment_ordering, keys, latent_up_weight)
    (relayed,) = attend((far,), scalars, segment_ordering, [q_far], lifted)
    got = turn(relayed, 1)
    direct, mine = attend((back, away), scalars, segment_ordering, [q_back, q_away], lifted)
    direct = turn(direct, -1)
    passed = turn(relay(got, mine), 1)
    (own,) = attend((near,), scalars, segment_ordering, [queries], lifted)
    return tuple(final(scalars, own, direct, passed, *pieces))


def solution(mesh):
    split = Mesh(mesh.devices.reshape(SIZES), AXES)
    ctx, tp = ("y", "x", "zh"), ("zl", "core")
    in_specs = (
        P(),
        P(ctx, tp),
        P(ctx + tp, None),
        P(ctx, tp),
        P(tp, None),
        P(tp, None),
        P(),
        P(),
        P(ctx, None),
        P(),
        P(None, tp),
    )
    out_specs = (P(ctx + tp, None), P(ctx, tp))
    return jax.shard_map(body, mesh=split, in_specs=in_specs, out_specs=out_specs, check_vma=False)
```

```python
import functools
import math

import jax
import jax.numpy as jnp
from jax import lax
from jax.experimental import pallas as pl
from jax.experimental.pallas import tpu as pltpu
from jax.sharding import Mesh, PartitionSpec as P

LATENT = 512
ROPE = 64
NOPE = 128
VDIM = 128
HEADS = 8
WIDE = 640
MESSAGE = HEADS * VDIM + 128
COLS = 896
BF = jnp.bfloat16
F32 = jnp.float32
MIB = 1 << 20
AXES = ("y", "x", "zh", "zl", "core")
SIZES = (4, 4, 2, 4, 2)
ORDER = (2, 1, 3, 0)


def dot(a, b):
    return jnp.dot(a, b, preferred_element_type=F32)


def shift(value, axis, k):
    return lax.ppermute(value, axis, [(i, (i + k) % 4) for i in range(4)])


def swap(value, axis, bit=1, size=2):
    return lax.ppermute(value, axis, [(i, i ^ bit) for i in range(size)])


def flat(y, x, zh, zl, core):
    return (((y * 4 + x) * 2 + zh) * 4 + zl) * 2 + core


def turn(value, k):
    perm = []
    for x in range(4):
        for core in range(2):
            perm.append((x * 2 + core, (x + (k if core == 0 else -k)) % 4 * 2 + core))
    return lax.ppermute(value, ("x", "core"), perm)


def tie(*values):
    return lax.optimization_barrier(values)


def near_block(value):
    same = ((1, 0), (1, 1), (2, 0), (2, 1))
    crossing = ((3, 0), (3, 1), (0, 0), (0, 1))
    perm = []
    for y in range(4):
        for x in range(4):
            for zh in range(2):
                for zl in range(4):
                    for core in range(2):
                        source = same[zl] if core == zh else crossing[zl]
                        perm.append((flat(y ^ zl, x, core, *source), flat(y, x, zh, zl, core)))
    return lax.ppermute(value, AXES, perm)


def cross(value):
    perm = [(zh * 4 + zl, (1 - zh) * 4 + (zl ^ 2)) for zh in range(2) for zl in range(4)]
    return lax.ppermute(value, ("zh", "zl"), perm)


def coords(s):
    f = s[0]
    return f // 64, f // 16 % 4, f // 8 % 2, f // 2 % 4, f % 2


def params(mib):
    return pltpu.CompilerParams(vmem_limit_bytes=int(mib * MIB))


def shape(dims, dtype=BF):
    return jax.ShapeDtypeStruct(dims, dtype)


def project_kernel(s, x_hbm, ad_hbm, w_hbm, au_hbm, res_hbm, send_ref, keep_ref, x, ad, w, au, res, xr, kept, sem):
    y, _, _, zl, core = coords(s)
    columns = [pl.ds(pl.multiple_of((y ^ ((zl + k) % 4)) * COLS, 128), COLS) for k in ORDER]

    def fetch(source, target, index):
        copy = pltpu.make_async_copy(source, target, sem.at[index])
        copy.start()
        return copy

    first = [fetch(x_hbm, x, 0), fetch(ad_hbm, ad, 1)]
    weights = [fetch(w_hbm.at[:, column], w.at[b], 4 + b) for b, column in enumerate(columns[:1])]
    second = [fetch(au_hbm, au, 2), fetch(res_hbm, res, 3)]
    weights += [fetch(w_hbm.at[:, column], w.at[b + 1], 5 + b) for b, column in enumerate(columns[1:])]
    for copy in first:
        copy.wait()
    xr[0:64, :] = x[:, 1 - core].reshape(64, 1024)
    xr[64:128, :] = x[:, core].reshape(64, 1024)
    down = dot(xr[...], ad[...])
    high = down.astype(BF)
    pieces = jnp.concatenate([high, (down - high.astype(F32)).astype(BF)], axis=0)
    rows = pl.ds(pl.multiple_of(zl * 16, 16), 16)
    for b, column in enumerate(columns):
        weights[b].wait()
        acc = dot(xr[...], w[b])
        if b == 0:
            for copy in second:
                copy.wait()
        adapter = dot(pieces, au[:, column])
        acc = acc + adapter[:128] + adapter[128:]
        send_ref[b] = acc[:64].astype(BF)
        kept[...] = acc[64:]
        kept[rows, :] = kept[rows, :] + res[:, column].astype(F32)
        keep_ref[b] = kept[...].astype(BF)


def project(scalars, *operands):
    return pl.pallas_call(
        project_kernel,
        in_specs=[pl.BlockSpec(memory_space=pltpu.SMEM)] + [pl.BlockSpec(memory_space=pltpu.HBM)] * 5,
        out_specs=[pl.BlockSpec(memory_space=pltpu.VMEM)] * 2,
        out_shape=[shape((4, 64, COLS))] * 2,
        scratch_shapes=[
            pltpu.VMEM((4, 2, 16, 1024), BF),
            pltpu.VMEM((1024, 256), BF),
            pltpu.VMEM((4, 1024, COLS), BF),
            pltpu.VMEM((256, 4 * COLS), BF),
            pltpu.VMEM((16, 4 * COLS), BF),
            pltpu.VMEM((128, 1024), BF),
            pltpu.VMEM((64, COLS), F32),
            pltpu.SemaphoreType.DMA((8,)),
        ],
        compiler_params=params(52.5),
        name="project",
    )(scalars, *operands)


def local(kernel, outs, mib, name, smem=0, vmem=0, scratch=()):
    space = lambda kind, n: [pl.BlockSpec(memory_space=kind)] * n
    out_specs = pl.BlockSpec(memory_space=pltpu.VMEM)
    return pl.pallas_call(
        kernel,
        in_specs=space(pltpu.SMEM, smem) + space(pltpu.VMEM, vmem),
        out_specs=[out_specs] * len(outs) if isinstance(outs, list) else out_specs,
        out_shape=outs,
        scratch_shapes=scratch,
        compiler_params=params(mib),
        name=name,
    )


def pair_sum_kernel(keep_ref, got_ref, *outs):
    for k, out in enumerate(outs):
        out[...] = (keep_ref[k].astype(F32) + got_ref[k].astype(F32)).astype(BF)


def pair_sum(keep, got, count):
    return local(pair_sum_kernel, [shape((64, COLS))] * count, 16, "pair_sum", vmem=2)(keep, got)


def pack_kernel(count, *refs):
    out_ref = refs[-1]
    start = 0
    for ref in refs[:count]:
        size = ref.shape[0]
        out_ref[start : start + size] = ref[...]
        start += size


def pack(blocks, after):
    dims = (sum(block.shape[0] for block in blocks),) + blocks[0].shape[1:]
    kernel = functools.partial(pack_kernel, len(blocks))
    return local(kernel, shape(dims), 16, "pack", vmem=len(blocks) + len(after))(*blocks, *after)


def assemble_kernel(s, own_ref, other_ref, out_ref):
    _, x, _, _, core = coords(s)
    out_ref[:, 512:] = jnp.zeros((COLS, WIDE - 512), BF)
    for k in range(4):
        for other, ref in enumerate((own_ref, other_ref)):
            zh = (core + other) % 2
            row = pl.multiple_of((x ^ k) * 224 + zh * 112, 16)
            out_ref[pl.ds(row, 112), 0:576] = ref[k]


def assemble(scalars, own, other):
    return local(assemble_kernel, shape((COLS, WIDE)), 16, "assemble", 1, 2)(scalars, own, other)


def tables_kernel(s, seg, cos_ref, sin_ref):
    y, x, zh, _, core = coords(s)
    ctx = y * 8 + x * 2 + zh
    row = lax.broadcasted_iota(jnp.int32, (64, ROPE), 0)
    lane = lax.broadcasted_iota(jnp.int32, (64, ROPE), 1)
    token = row // 16 * 32 + core * 16 + row % 16
    places = jnp.where(token < 64, seg[2 * ctx], seg[2 * ctx + 1]) * 64 + token % 64
    inverse = jnp.exp((lane % 32).astype(F32) * (-2.0 * math.log(10000.0) / ROPE))
    angles = places.astype(F32) * inverse
    cos_ref[...] = jnp.cos(angles)
    sine = jnp.sin(angles)
    sin_ref[...] = jnp.where(lane < 32, -sine, sine)


def tables(scalars, seg):
    return local(tables_kernel, [shape((64, ROPE), F32)] * 2, 16, "tables", 2)(scalars, seg)


def latent_kernel(s, keep_ref, got_ref, r1, r2, r3, gain_ref, w_ref, part_ref, h0, h1, h2, h3, hid):
    y, _, _, zl, _ = coords(s)
    total = sum(ref[...].astype(F32) for ref in (keep_ref.at[3], got_ref.at[3], r1, r2, r3))
    hidden = total.astype(BF)
    hid[...] = hidden
    for k, out in enumerate((h0, h1, h2, h3)):
        out[...] = hid[pl.ds(pl.multiple_of(((zl + k) % 4) * 16, 16), 16), :]
    wide = hidden.astype(F32)
    squares = jnp.sum(wide * wide, axis=1, keepdims=True)
    gain = gain_ref[:, pl.ds(pl.multiple_of((y ^ zl) * COLS, 128), COLS)].astype(F32)
    part = dot((wide * gain).astype(BF), w_ref[...])
    lane = lax.broadcasted_iota(jnp.int32, (64, 128), 1)
    high = squares.astype(BF).astype(F32)
    tail = jnp.where(lane == 64, high, jnp.where(lane == 65, squares - high, part[:, 512:]))
    part_ref[:, :512] = part[:, :512].astype(BF)
    part_ref[:, 512:] = tail.astype(BF)


def latent_part(scalars, *operands):
    outs = [shape((64, WIDE))] + [shape((16, COLS))] * 4
    scratch = [pltpu.VMEM((64, COLS), BF)]
    return local(latent_kernel, outs, 16, "latent_part", 1, 7, scratch)(scalars, *operands)


def rows_kernel(p0, p1, p2, p3, cos_ref, sin_ref, gain_ref, out_ref):
    total = p0[...].astype(F32) + p1[...].astype(F32) + p2[...].astype(F32) + p3[...].astype(F32)
    tail = total[:, 512:]
    inverse = lax.rsqrt((tail[:, 64:65] + tail[:, 65:66]) / 3584.0 + 1e-06)
    latent = total[:, :512] * inverse
    mean_square = jnp.mean(latent * latent, axis=1, keepdims=True)
    out_ref[:, :512] = (latent * lax.rsqrt(mean_square + 1e-06) * gain_ref[...].astype(F32)).astype(BF)
    rope = tail[:, :64] * inverse
    swapped = jnp.concatenate([rope[:, 32:], rope[:, :32]], axis=1)
    rotated = rope * cos_ref[...] + swapped * sin_ref[...]
    out_ref[:, 512:] = jnp.concatenate([rotated, jnp.zeros((64, 64), F32)], axis=1).astype(BF)


def kv_rows(parts, cosine, sine, gain):
    return local(rows_kernel, shape((64, WIDE)), 16, "kv_rows", vmem=7)(*parts, cosine, sine, gain)


def lift_kernel(s, seg, *refs):
    keys = refs[:8]
    up_ref, key_ref, value_ref, rope_ref, kv = refs[8:]
    y, x, zh, _, _ = coords(s)
    for k in range(4):
        for a in range(2):
            ctx = ((y + k) % 4) * 8 + x * 2 + (zh + a) % 2
            first_upper = (seg[2 * ctx] > seg[2 * ctx + 1]).astype(jnp.int32)
            for half in range(2):
                upper = first_upper if half == 0 else 1 - first_upper
                for other in range(2):
                    row = pl.multiple_of(upper * 512 + (k * 2 + a) * 64 + other * 32, 32)
                    start = a * 64 + half * 32
                    kv[pl.ds(row, 32), :] = keys[4 * other + k][start : start + 32, :]
    rope_ref[...] = kv[:, LATENT:]
    for head in range(HEADS):
        lifted = dot(kv[:, :LATENT], up_ref[:, head * 256 : head * 256 + 256]).astype(BF)
        key_ref[head] = lifted[:, :NOPE]
        value_ref[head] = lifted[:, NOPE:]


def lift(scalars, seg, keys, up):
    outs = [shape((HEADS, 1024, 128))] * 2 + [shape((1024, 128))]
    scratch = [pltpu.VMEM((1024, WIDE), BF)]
    return local(lift_kernel, outs, 24, "lift", 2, 9, scratch)(scalars, seg, *keys, up)


def stat_pieces(level, lane):
    high = level.astype(BF).astype(F32)
    middle = (level - high).astype(BF).astype(F32)
    return jnp.where(lane < 8, high, jnp.where(lane < 16, middle, level - high - middle))


def attend_kernel(chunks, s, seg, *refs):
    count = len(chunks)
    queries = refs[:count]
    key_ref, value_ref, rope_ref = refs[count : count + 3]
    outs = refs[count + 3 :]
    y, x, zh, _, core = coords(s)
    hops = (0, 1 + 2 * core, 2, 3 - 2 * core)
    factor = math.log2(math.e) / math.sqrt(NOPE + ROPE)
    lane = lax.broadcasted_iota(jnp.int32, (1, 512), 1)
    lower = jnp.zeros((1, 512), jnp.int32)
    upper = lower
    for k in range(4):
        for a in range(2):
            ctx = ((y + k) % 4) * 8 + x * 2 + (zh + a) % 2
            one, two = seg[2 * ctx], seg[2 * ctx + 1]
            lower = jnp.where(lane // 64 == k * 2 + a, jnp.minimum(one, two), lower)
            upper = jnp.where(lane // 64 == k * 2 + a, jnp.maximum(one, two), upper)
    inside = (lane // 16) % 2 * 32 + ((lane // 32) % 2 + core) % 2 * 16 + lane % 16
    row = lax.broadcasted_iota(jnp.int32, (64, 512), 0)
    low_rows, high_rows, low_bias, high_bias = [], [], [], []
    for chunk in chunks:
        ctx = y * 8 + ((x + hops[chunk]) % 4) * 2 + zh
        one, two = seg[2 * ctx], seg[2 * ctx + 1]
        flipped = (one > two).astype(jnp.int32)
        low_rows.append(pl.ds(pl.multiple_of(flipped * 64, 64), 64))
        high_rows.append(pl.ds(pl.multiple_of(64 - flipped * 64, 64), 64))
        low_bias.append(jnp.where(lower * 64 + inside <= row + jnp.minimum(one, two) * 64, 0.0, -1e30))
        high_bias.append(jnp.where(upper * 64 + inside <= row + jnp.maximum(one, two) * 64, 0.0, -1e30))
    low_bias = jnp.concatenate(low_bias, axis=0)
    high_bias = jnp.concatenate(high_bias, axis=0)
    rows = 64 * count
    stat_lane = lax.broadcasted_iota(jnp.int32, (2 * rows, 128), 1)
    stats = jnp.zeros((2 * rows, 128), F32)
    across = (((1,), (1,)), ((), ()))
    ones = jnp.ones((512, 128), BF)
    wide_key = lambda h, part: jnp.concatenate([key_ref[h, part, :], rope_ref[part, :]], axis=1)
    wide_value = lambda h, part: jnp.concatenate([value_ref[h, part, :], ones], axis=1)
    lows, highs = slice(0, 512), slice(512, 1024)
    near, far = [], []
    for head in range(HEADS):
        column = slice(head * 192, head * 192 + 192)
        pieces = [q[r, column] for q, r in zip(queries, low_rows)] + [q[r, column] for q, r in zip(queries, high_rows)]
        query = jnp.concatenate([jnp.concatenate(pieces, axis=0), jnp.zeros((2 * rows, 64), BF)], axis=1)
        near.append(lax.dot_general(query, wide_key(head, lows), across, preferred_element_type=F32))
        high = lax.dot_general(query[rows:], wide_key(head, highs), across, preferred_element_type=F32)
        far.append(high + high_bias)
    low = [scores[:rows] + low_bias for scores in near]
    mid = [scores[rows:] for scores in near]
    low_top = [jnp.max(scores, axis=1, keepdims=True) for scores in low]
    high_top = [jnp.max(jnp.maximum(a, b), axis=1, keepdims=True) for a, b in zip(mid, far)]
    weigh = lambda scores, top: jnp.exp2((scores - top) * factor).astype(BF)
    low = [weigh(a, t) for a, t in zip(low, low_top)]
    mid = [weigh(a, t) for a, t in zip(mid, high_top)]
    far = [weigh(a, t) for a, t in zip(far, high_top)]
    first = [dot(jnp.concatenate([a, b], axis=0), wide_value(h, lows)) for h, (a, b) in enumerate(zip(low, mid))]
    second = [dot(a, wide_value(h, highs)) for h, a in enumerate(far)]
    for head in range(HEADS):
        both = jnp.concatenate([first[head][:rows], first[head][rows:] + second[head]], axis=0)
        top = jnp.concatenate([low_top[head], high_top[head]], axis=0)
        mixed = (both[:, :VDIM] / both[:, VDIM:]).astype(BF)
        level = top * factor + jnp.log2(both[:, VDIM:])
        stats = jnp.where(stat_lane % 8 == head, level, stats)
        for c in range(count):
            column = slice(head * 128, head * 128 + 128)
            outs[c][low_rows[c], column] = mixed[64 * c : 64 * c + 64]
            outs[c][high_rows[c], column] = mixed[rows + 64 * c : rows + 64 * c + 64]
    stats = jnp.where(stat_lane < 24, stat_pieces(stats, stat_lane), 0.0).astype(BF)
    for c in range(count):
        outs[c][low_rows[c], HEADS * 128 :] = stats[64 * c : 64 * c + 64]
        outs[c][high_rows[c], HEADS * 128 :] = stats[rows + 64 * c : rows + 64 * c + 64]


def attend(chunks, scalars, seg, queries, lifted):
    kernel = functools.partial(attend_kernel, chunks)
    outs = [shape((128, MESSAGE))] * len(chunks)
    return local(kernel, outs, 32, "attend", 2, len(chunks) + 3)(scalars, seg, *queries, *lifted)


def spread_levels(ref, width, group):
    row = lax.broadcasted_iota(jnp.int32, (128, width), 0)
    lane = lax.broadcasted_iota(jnp.int32, (128, width), 1)
    picks = (row < 24) & (row % 8 == (lane // group) % 8)
    return dot(ref[:, HEADS * 128 :], picks.astype(F32).astype(BF))


def merged(refs):
    levels = [spread_levels(ref, 1024, 128) for ref in refs]
    top = functools.reduce(jnp.maximum, levels)
    scales = [jnp.exp2(level - top) for level in levels]
    mixed = sum(ref[:, : HEADS * 128].astype(F32) * scale for ref, scale in zip(refs, scales))
    return (mixed / sum(scales[1:], scales[0])).astype(BF)


def relay_kernel(got_ref, own_ref, out_ref):
    refs = (got_ref, own_ref)
    out_ref[:, : HEADS * 128] = merged(refs)
    one, two = [spread_levels(ref, 128, 1) for ref in refs]
    top = jnp.maximum(one, two)
    level = top + jnp.log2(jnp.exp2(one - top) + jnp.exp2(two - top))
    lane = lax.broadcasted_iota(jnp.int32, (128, 128), 1)
    out_ref[:, HEADS * 128 :] = jnp.where(lane < 24, stat_pieces(level, lane), 0.0).astype(BF)


def relay(got, own):
    return local(relay_kernel, shape((128, MESSAGE)), 16, "relay", vmem=2)(got, own)


def final_kernel(s, a_ref, b_ref, c_ref, h0, h1, h2, h3, hidden_ref, attn_ref):
    y, _, _, zl, _ = coords(s)
    for k, ref in enumerate((h0, h1, h2, h3)):
        column = pl.multiple_of((y ^ ((zl + 4 - k) % 4)) * COLS, 128)
        hidden_ref[:, pl.ds(column, COLS)] = ref[...]
    attn_ref[...] = merged((a_ref, b_ref, c_ref))


def final(scalars, *operands):
    outs = [shape((16, 4 * COLS)), shape((128, HEADS * VDIM))]
    return local(final_kernel, outs, 16, "final", 1, 7)(scalars, *operands)


def body(
    segment_ordering,
    attention_input,
    residual,
    queries,
    output_weight,
    adapter_down_factor,
    adapter_up_factor,
    input_norm_gain,
    latent_key_weight,
    latent_norm_gain,
    latent_up_weight,
):
    scalars = lax.axis_index(AXES).astype(jnp.int32).reshape(1)
    near, away, far, back = 0, 1, 2, 3

    block = near_block(latent_key_weight)[None]
    send, keep = project(
        scalars,
        attention_input.reshape(4, 2, 16, 1024),
        adapter_down_factor,
        output_weight,
        adapter_up_factor,
        residual,
    )
    block, send = tie(block, send)
    got = swap(send, "core")
    blocks = [block] + [swap(block, "x", k, 4) for k in (1, 2, 3)]
    sums = pair_sum(keep, got, 3)
    r2, r1, r3 = (shift(value, "zl", k) for value, k in zip(sums, ORDER))
    four = pack(blocks, (r1, r2, r3))
    weight = assemble(scalars, four, swap(four, "core"))
    q_far, q_back = shift(queries, "x", 2), turn(queries, 1)
    q_away = turn(tie(queries, q_far)[0], -1)
    part, h0, h1, h2, h3 = latent_part(
        scalars, keep, got, r1, r2, r3, input_norm_gain.reshape(1, -1), weight
    )
    cosine, sine = tables(scalars, tie(segment_ordering, part)[0])
    p1, p2, p3 = (shift(part, "zl", k) for k in (1, 2, 3))
    rows = kv_rows([part, p1, p2, p3], cosine, sine, latent_norm_gain.reshape(1, -1))
    rows, h1, h2, h3 = tie(rows, h1, h2, h3)
    beside = cross(rows)
    pieces = [h0] + [shift(h, "zl", k) for k, h in ((1, h1), (2, h2), (3, h3))]
    both = pack([rows, beside], (q_far,))
    column = [both] + [shift(both, "y", -k) for k in (1, 2, 3)]
    keys = column + [swap(value, "core") for value in column]

    *keys, q_back, q_away = tie(*keys, q_back, q_away)
    lifted = lift(scalars, segment_ordering, keys, latent_up_weight)
    (relayed,) = attend((far,), scalars, segment_ordering, [q_far], lifted)
    got = turn(relayed, 1)
    direct, mine = attend((back, away), scalars, segment_ordering, [q_back, q_away], lifted)
    direct = turn(direct, -1)
    passed = turn(relay(got, mine), 1)
    (own,) = attend((near,), scalars, segment_ordering, [queries], lifted)
    return tuple(final(scalars, own, direct, passed, *pieces))


def solution(mesh):
    split = Mesh(mesh.devices.reshape(SIZES), AXES)
    ctx, tp = ("y", "x", "zh"), ("zl", "core")
    in_specs = (
        P(),
        P(ctx, tp),
        P(ctx + tp, None),
        P(ctx, tp),
        P(tp, None),
        P(tp, None),
        P(),
        P(),
        P(ctx, None),
        P(),
        P(None, tp),
    )
    out_specs = (P(ctx + tp, None), P(ctx, tp))
    return jax.shard_map(body, mesh=split, in_specs=in_specs, out_specs=out_specs, check_vma=False)
```

```python
import functools
import math

import jax
import jax.numpy as jnp
from jax import lax
from jax.experimental import pallas as pl
from jax.experimental.pallas import tpu as pltpu
from jax.sharding import Mesh, PartitionSpec as P

LATENT = 512
ROPE = 64
NOPE = 128
VDIM = 128
HEADS = 8
WIDE = 640
MESSAGE = HEADS * VDIM + 128
COLS = 896
BF = jnp.bfloat16
F32 = jnp.float32
MIB = 1 << 20
AXES = ("y", "x", "zh", "zl", "core")
SIZES = (4, 4, 2, 4, 2)
ORDER = (2, 1, 3, 0)


def dot(a, b):
    return jnp.dot(a, b, preferred_element_type=F32)


def shift(value, axis, k):
    return lax.ppermute(value, axis, [(i, (i + k) % 4) for i in range(4)])


def swap(value, axis, bit=1, size=2):
    return lax.ppermute(value, axis, [(i, i ^ bit) for i in range(size)])


def flat(y, x, zh, zl, core):
    return (((y * 4 + x) * 2 + zh) * 4 + zl) * 2 + core


def turn(value, k):
    perm = []
    for x in range(4):
        for core in range(2):
            perm.append((x * 2 + core, (x + (k if core == 0 else -k)) % 4 * 2 + core))
    return lax.ppermute(value, ("x", "core"), perm)


def tie(*values):
    return lax.optimization_barrier(values)


def near_block(value):
    same = ((1, 0), (1, 1), (2, 0), (2, 1))
    crossing = ((3, 0), (3, 1), (0, 0), (0, 1))
    perm = []
    for y in range(4):
        for x in range(4):
            for zh in range(2):
                for zl in range(4):
                    for core in range(2):
                        source = same[zl] if core == zh else crossing[zl]
                        perm.append((flat(y ^ zl, x, core, *source), flat(y, x, zh, zl, core)))
    return lax.ppermute(value, AXES, perm)


def cross(value):
    perm = [(zh * 4 + zl, (1 - zh) * 4 + (zl ^ 2)) for zh in range(2) for zl in range(4)]
    return lax.ppermute(value, ("zh", "zl"), perm)


def coords(s):
    f = s[0]
    return f // 64, f // 16 % 4, f // 8 % 2, f // 2 % 4, f % 2


def params(mib):
    return pltpu.CompilerParams(vmem_limit_bytes=int(mib * MIB))


def shape(dims, dtype=BF):
    return jax.ShapeDtypeStruct(dims, dtype)


def project_kernel(s, x_hbm, ad_hbm, w_hbm, au_hbm, res_hbm, send_ref, keep_ref, x, ad, w, au, res, xr, kept, sem):
    y, _, _, zl, core = coords(s)
    columns = [pl.ds(pl.multiple_of((y ^ ((zl + k) % 4)) * COLS, 128), COLS) for k in ORDER]

    def fetch(source, target, index):
        copy = pltpu.make_async_copy(source, target, sem.at[index])
        copy.start()
        return copy

    first = [fetch(x_hbm, x, 0), fetch(ad_hbm, ad, 1)]
    weights = [fetch(w_hbm.at[:, column], w.at[b], 4 + b) for b, column in enumerate(columns[:1])]
    second = [fetch(au_hbm, au, 2), fetch(res_hbm, res, 3)]
    weights += [fetch(w_hbm.at[:, column], w.at[b + 1], 5 + b) for b, column in enumerate(columns[1:])]
    for copy in first:
        copy.wait()
    xr[0:64, :] = x[:, 1 - core].reshape(64, 1024)
    xr[64:128, :] = x[:, core].reshape(64, 1024)
    down = dot(xr[...], ad[...])
    high = down.astype(BF)
    pieces = jnp.concatenate([high, (down - high.astype(F32)).astype(BF)], axis=0)
    rows = pl.ds(pl.multiple_of(zl * 16, 16), 16)
    for b, column in enumerate(columns):
        weights[b].wait()
        acc = dot(xr[...], w[b])
        if b == 0:
            for copy in second:
                copy.wait()
        adapter = dot(pieces, au[:, column])
        acc = acc + adapter[:128] + adapter[128:]
        send_ref[b] = acc[:64].astype(BF)
        kept[...] = acc[64:]
        kept[rows, :] = kept[rows, :] + res[:, column].astype(F32)
        keep_ref[b] = kept[...].astype(BF)


def project(scalars, *operands):
    return pl.pallas_call(
        project_kernel,
        in_specs=[pl.BlockSpec(memory_space=pltpu.SMEM)] + [pl.BlockSpec(memory_space=pltpu.HBM)] * 5,
        out_specs=[pl.BlockSpec(memory_space=pltpu.VMEM)] * 2,
        out_shape=[shape((4, 64, COLS))] * 2,
        scratch_shapes=[
            pltpu.VMEM((4, 2, 16, 1024), BF),
            pltpu.VMEM((1024, 256), BF),
            pltpu.VMEM((4, 1024, COLS), BF),
            pltpu.VMEM((256, 4 * COLS), BF),
            pltpu.VMEM((16, 4 * COLS), BF),
            pltpu.VMEM((128, 1024), BF),
            pltpu.VMEM((64, COLS), F32),
            pltpu.SemaphoreType.DMA((8,)),
        ],
        compiler_params=params(52.5),
        name="project",
    )(scalars, *operands)


def local(kernel, outs, mib, name, smem=0, vmem=0, scratch=()):
    space = lambda kind, n: [pl.BlockSpec(memory_space=kind)] * n
    out_specs = pl.BlockSpec(memory_space=pltpu.VMEM)
    return pl.pallas_call(
        kernel,
        in_specs=space(pltpu.SMEM, smem) + space(pltpu.VMEM, vmem),
        out_specs=[out_specs] * len(outs) if isinstance(outs, list) else out_specs,
        out_shape=outs,
        scratch_shapes=scratch,
        compiler_params=params(mib),
        name=name,
    )


def pair_sum_kernel(keep_ref, got_ref, *outs):
    for k, out in enumerate(outs):
        out[...] = (keep_ref[k].astype(F32) + got_ref[k].astype(F32)).astype(BF)


def pair_sum(keep, got, count):
    return local(pair_sum_kernel, [shape((64, COLS))] * count, 16, "pair_sum", vmem=2)(keep, got)


def pack_kernel(count, *refs):
    out_ref = refs[-1]
    start = 0
    for ref in refs[:count]:
        size = ref.shape[0]
        out_ref[start : start + size] = ref[...]
        start += size


def pack(blocks, after):
    dims = (sum(block.shape[0] for block in blocks),) + blocks[0].shape[1:]
    kernel = functools.partial(pack_kernel, len(blocks))
    return local(kernel, shape(dims), 16, "pack", vmem=len(blocks) + len(after))(*blocks, *after)


def assemble_kernel(s, own_ref, other_ref, out_ref):
    _, x, _, _, core = coords(s)
    out_ref[:, 512:] = jnp.zeros((COLS, WIDE - 512), BF)
    for k in range(4):
        for other, ref in enumerate((own_ref, other_ref)):
            zh = (core + other) % 2
            row = pl.multiple_of((x ^ k) * 224 + zh * 112, 16)
            out_ref[pl.ds(row, 112), 0:576] = ref[k]


def assemble(scalars, own, other):
    return local(assemble_kernel, shape((COLS, WIDE)), 16, "assemble", 1, 2)(scalars, own, other)


def tables_kernel(s, seg, cos_ref, sin_ref):
    y, x, zh, _, core = coords(s)
    ctx = y * 8 + x * 2 + zh
    row = lax.broadcasted_iota(jnp.int32, (64, ROPE), 0)
    lane = lax.broadcasted_iota(jnp.int32, (64, ROPE), 1)
    token = row // 16 * 32 + core * 16 + row % 16
    places = jnp.where(token < 64, seg[2 * ctx], seg[2 * ctx + 1]) * 64 + token % 64
    inverse = jnp.exp((lane % 32).astype(F32) * (-2.0 * math.log(10000.0) / ROPE))
    angles = places.astype(F32) * inverse
    cos_ref[...] = jnp.cos(angles)
    sine = jnp.sin(angles)
    sin_ref[...] = jnp.where(lane < 32, -sine, sine)


def tables(scalars, seg):
    return local(tables_kernel, [shape((64, ROPE), F32)] * 2, 16, "tables", 2)(scalars, seg)


def latent_kernel(s, keep_ref, got_ref, r1, r2, r3, gain_ref, w_ref, part_ref, h0, h1, h2, h3, hid):
    y, _, _, zl, _ = coords(s)
    total = sum(ref[...].astype(F32) for ref in (keep_ref.at[3], got_ref.at[3], r1, r2, r3))
    hidden = total.astype(BF)
    hid[...] = hidden
    for k, out in enumerate((h0, h1, h2, h3)):
        out[...] = hid[pl.ds(pl.multiple_of(((zl + k) % 4) * 16, 16), 16), :]
    wide = hidden.astype(F32)
    squares = jnp.sum(wide * wide, axis=1, keepdims=True)
    gain = gain_ref[:, pl.ds(pl.multiple_of((y ^ zl) * COLS, 128), COLS)].astype(F32)
    part = dot((wide * gain).astype(BF), w_ref[...])
    lane = lax.broadcasted_iota(jnp.int32, (64, 128), 1)
    high = squares.astype(BF).astype(F32)
    tail = jnp.where(lane == 64, high, jnp.where(lane == 65, squares - high, part[:, 512:]))
    part_ref[:, :512] = part[:, :512].astype(BF)
    part_ref[:, 512:] = tail.astype(BF)


def latent_part(scalars, *operands):
    outs = [shape((64, WIDE))] + [shape((16, COLS))] * 4
    scratch = [pltpu.VMEM((64, COLS), BF)]
    return local(latent_kernel, outs, 16, "latent_part", 1, 7, scratch)(scalars, *operands)


def rows_kernel(p0, p1, p2, p3, cos_ref, sin_ref, gain_ref, out_ref):
    total = p0[...].astype(F32) + p1[...].astype(F32) + p2[...].astype(F32) + p3[...].astype(F32)
    tail = total[:, 512:]
    inverse = lax.rsqrt((tail[:, 64:65] + tail[:, 65:66]) / 3584.0 + 1e-06)
    latent = total[:, :512] * inverse
    mean_square = jnp.mean(latent * latent, axis=1, keepdims=True)
    out_ref[:, :512] = (latent * lax.rsqrt(mean_square + 1e-06) * gain_ref[...].astype(F32)).astype(BF)
    rope = tail[:, :64] * inverse
    swapped = jnp.concatenate([rope[:, 32:], rope[:, :32]], axis=1)
    rotated = rope * cos_ref[...] + swapped * sin_ref[...]
    out_ref[:, 512:] = jnp.concatenate([rotated, jnp.zeros((64, 64), F32)], axis=1).astype(BF)


def kv_rows(parts, cosine, sine, gain):
    return local(rows_kernel, shape((64, WIDE)), 16, "kv_rows", vmem=7)(*parts, cosine, sine, gain)


def lift_kernel(s, seg, *refs):
    keys = refs[:8]
    up_ref, key_ref, value_ref, rope_ref, kv = refs[8:]
    y, x, zh, _, _ = coords(s)
    for k in range(4):
        for a in range(2):
            ctx = ((y + k) % 4) * 8 + x * 2 + (zh + a) % 2
            first_upper = (seg[2 * ctx] > seg[2 * ctx + 1]).astype(jnp.int32)
            for half in range(2):
                upper = first_upper if half == 0 else 1 - first_upper
                for other in range(2):
                    row = pl.multiple_of(upper * 512 + (k * 2 + a) * 64 + other * 32, 32)
                    start = a * 64 + half * 32
                    kv[pl.ds(row, 32), :] = keys[4 * other + k][start : start + 32, :]
    rope_ref[...] = kv[:, LATENT:]
    for head in range(HEADS):
        lifted = dot(kv[:, :LATENT], up_ref[:, head * 256 : head * 256 + 256]).astype(BF)
        key_ref[head] = lifted[:, :NOPE]
        value_ref[head] = lifted[:, NOPE:]


def lift(scalars, seg, keys, up):
    outs = [shape((HEADS, 1024, 128))] * 2 + [shape((1024, 128))]
    scratch = [pltpu.VMEM((1024, WIDE), BF)]
    return local(lift_kernel, outs, 24, "lift", 2, 9, scratch)(scalars, seg, *keys, up)


def stat_pieces(level, lane):
    high = level.astype(BF).astype(F32)
    middle = (level - high).astype(BF).astype(F32)
    return jnp.where(lane < 8, high, jnp.where(lane < 16, middle, level - high - middle))


def attend_kernel(chunks, s, seg, *refs):
    count = len(chunks)
    queries = refs[:count]
    key_ref, value_ref, rope_ref = refs[count : count + 3]
    outs = refs[count + 3 :]
    y, x, zh, _, core = coords(s)
    hops = (0, 1 + 2 * core, 2, 3 - 2 * core)
    factor = math.log2(math.e) / math.sqrt(NOPE + ROPE)
    lane = lax.broadcasted_iota(jnp.int32, (1, 512), 1)
    lower = jnp.zeros((1, 512), jnp.int32)
    upper = lower
    for k in range(4):
        for a in range(2):
            ctx = ((y + k) % 4) * 8 + x * 2 + (zh + a) % 2
            one, two = seg[2 * ctx], seg[2 * ctx + 1]
            lower = jnp.where(lane // 64 == k * 2 + a, jnp.minimum(one, two), lower)
            upper = jnp.where(lane // 64 == k * 2 + a, jnp.maximum(one, two), upper)
    inside = (lane // 16) % 2 * 32 + ((lane // 32) % 2 + core) % 2 * 16 + lane % 16
    row = lax.broadcasted_iota(jnp.int32, (64, 512), 0)
    low_rows, high_rows, low_bias, high_bias = [], [], [], []
    for chunk in chunks:
        ctx = y * 8 + ((x + hops[chunk]) % 4) * 2 + zh
        one, two = seg[2 * ctx], seg[2 * ctx + 1]
        flipped = (one > two).astype(jnp.int32)
        low_rows.append(pl.ds(pl.multiple_of(flipped * 64, 64), 64))
        high_rows.append(pl.ds(pl.multiple_of(64 - flipped * 64, 64), 64))
        low_bias.append(jnp.where(lower * 64 + inside <= row + jnp.minimum(one, two) * 64, 0.0, -1e30))
        high_bias.append(jnp.where(upper * 64 + inside <= row + jnp.maximum(one, two) * 64, 0.0, -1e30))
    low_bias = jnp.concatenate(low_bias, axis=0)
    high_bias = jnp.concatenate(high_bias, axis=0)
    rows = 64 * count
    stat_lane = lax.broadcasted_iota(jnp.int32, (2 * rows, 128), 1)
    stats = jnp.zeros((2 * rows, 128), F32)
    across = (((1,), (1,)), ((), ()))
    ones = jnp.ones((512, 128), BF)
    wide_key = lambda h, part: jnp.concatenate([key_ref[h, part, :], rope_ref[part, :]], axis=1)
    wide_value = lambda h, part: jnp.concatenate([value_ref[h, part, :], ones], axis=1)
    lows, highs = slice(0, 512), slice(512, 1024)
    near, far = [], []
    for head in range(HEADS):
        column = slice(head * 192, head * 192 + 192)
        pieces = [q[r, column] for q, r in zip(queries, low_rows)] + [q[r, column] for q, r in zip(queries, high_rows)]
        query = jnp.concatenate([jnp.concatenate(pieces, axis=0), jnp.zeros((2 * rows, 64), BF)], axis=1)
        near.append(lax.dot_general(query, wide_key(head, lows), across, preferred_element_type=F32))
        high = lax.dot_general(query[rows:], wide_key(head, highs), across, preferred_element_type=F32)
        far.append(high + high_bias)
    low = [scores[:rows] + low_bias for scores in near]
    mid = [scores[rows:] for scores in near]
    low_top = [jnp.max(scores, axis=1, keepdims=True) for scores in low]
    high_top = [jnp.max(jnp.maximum(a, b), axis=1, keepdims=True) for a, b in zip(mid, far)]
    weigh = lambda scores, top: jnp.exp2((scores - top) * factor).astype(BF)
    low = [weigh(a, t) for a, t in zip(low, low_top)]
    mid = [weigh(a, t) for a, t in zip(mid, high_top)]
    far = [weigh(a, t) for a, t in zip(far, high_top)]
    first = [dot(jnp.concatenate([a, b], axis=0), wide_value(h, lows)) for h, (a, b) in enumerate(zip(low, mid))]
    second = [dot(a, wide_value(h, highs)) for h, a in enumerate(far)]
    for head in range(HEADS):
        both = jnp.concatenate([first[head][:rows], first[head][rows:] + second[head]], axis=0)
        top = jnp.concatenate([low_top[head], high_top[head]], axis=0)
        mixed = (both[:, :VDIM] / both[:, VDIM:]).astype(BF)
        level = top * factor + jnp.log2(both[:, VDIM:])
        stats = jnp.where(stat_lane % 8 == head, level, stats)
        for c in range(count):
            column = slice(head * 128, head * 128 + 128)
            outs[c][low_rows[c], column] = mixed[64 * c : 64 * c + 64]
            outs[c][high_rows[c], column] = mixed[rows + 64 * c : rows + 64 * c + 64]
    stats = jnp.where(stat_lane < 24, stat_pieces(stats, stat_lane), 0.0).astype(BF)
    for c in range(count):
        outs[c][low_rows[c], HEADS * 128 :] = stats[64 * c : 64 * c + 64]
        outs[c][high_rows[c], HEADS * 128 :] = stats[rows + 64 * c : rows + 64 * c + 64]


def attend(chunks, scalars, seg, queries, lifted):
    kernel = functools.partial(attend_kernel, chunks)
    outs = [shape((128, MESSAGE))] * len(chunks)
    return local(kernel, outs, 32, "attend", 2, len(chunks) + 3)(scalars, seg, *queries, *lifted)


def spread_levels(ref, width, group):
    row = lax.broadcasted_iota(jnp.int32, (128, width), 0)
    lane = lax.broadcasted_iota(jnp.int32, (128, width), 1)
    picks = (row < 24) & (row % 8 == (lane // group) % 8)
    return dot(ref[:, HEADS * 128 :], picks.astype(F32).astype(BF))


def merged(refs):
    levels = [spread_levels(ref, 1024, 128) for ref in refs]
    top = functools.reduce(jnp.maximum, levels)
    scales = [jnp.exp2(level - top) for level in levels]
    mixed = sum(ref[:, : HEADS * 128].astype(F32) * scale for ref, scale in zip(refs, scales))
    return (mixed / sum(scales[1:], scales[0])).astype(BF)


def relay_kernel(got_ref, own_ref, out_ref):
    refs = (got_ref, own_ref)
    out_ref[:, : HEADS * 128] = merged(refs)
    one, two = [spread_levels(ref, 128, 1) for ref in refs]
    top = jnp.maximum(one, two)
    level = top + jnp.log2(jnp.exp2(one - top) + jnp.exp2(two - top))
    lane = lax.broadcasted_iota(jnp.int32, (128, 128), 1)
    out_ref[:, HEADS * 128 :] = jnp.where(lane < 24, stat_pieces(level, lane), 0.0).astype(BF)


def relay(got, own):
    return local(relay_kernel, shape((128, MESSAGE)), 16, "relay", vmem=2)(got, own)


def final_kernel(s, a_ref, b_ref, c_ref, h0, h1, h2, h3, hidden_ref, attn_ref):
    y, _, _, zl, _ = coords(s)
    for k, ref in enumerate((h0, h1, h2, h3)):
        column = pl.multiple_of((y ^ ((zl + 4 - k) % 4)) * COLS, 128)
        hidden_ref[:, pl.ds(column, COLS)] = ref[...]
    attn_ref[...] = merged((a_ref, b_ref, c_ref))


def final(scalars, *operands):
    outs = [shape((16, 4 * COLS)), shape((128, HEADS * VDIM))]
    return local(final_kernel, outs, 16, "final", 1, 7)(scalars, *operands)


def body(
    segment_ordering,
    attention_input,
    residual,
    queries,
    output_weight,
    adapter_down_factor,
    adapter_up_factor,
    input_norm_gain,
    latent_key_weight,
    latent_norm_gain,
    latent_up_weight,
):
    scalars = lax.axis_index(AXES).astype(jnp.int32).reshape(1)
    near, away, far, back = 0, 1, 2, 3

    block = near_block(latent_key_weight)[None]
    send, keep = project(
        scalars,
        attention_input.reshape(4, 2, 16, 1024),
        adapter_down_factor,
        output_weight,
        adapter_up_factor,
        residual,
    )
    block, send = tie(block, send)
    got = swap(send, "core")
    sums = pair_sum(keep, got, 3)
    late = pack([block], sums[:1])
    blocks = [block, swap(block, "x", 1, 4), swap(late, "x", 2, 4), swap(block, "x", 3, 4)]
    r2, r1, r3 = (shift(value, "zl", k) for value, k in zip(sums, ORDER))
    four = pack(blocks, (r1, r2, r3))
    weight = assemble(scalars, four, swap(four, "core"))
    q_far, q_back = shift(queries, "x", 2), turn(queries, 1)
    q_away = turn(tie(queries, q_far)[0], -1)
    part, h0, h1, h2, h3 = latent_part(
        scalars, keep, got, r1, r2, r3, input_norm_gain.reshape(1, -1), weight
    )
    cosine, sine = tables(scalars, tie(segment_ordering, part)[0])
    p1, p2, p3 = (shift(part, "zl", k) for k in (1, 2, 3))
    rows = kv_rows([part, p1, p2, p3], cosine, sine, latent_norm_gain.reshape(1, -1))
    rows, h1, h2, h3 = tie(rows, h1, h2, h3)
    beside = cross(rows)
    pieces = [h0] + [shift(h, "zl", k) for k, h in ((1, h1), (2, h2), (3, h3))]
    both = pack([rows, beside], (q_far,))
    column = [both] + [shift(both, "y", -k) for k in (1, 2, 3)]
    keys = column + [swap(value, "core") for value in column]

    *keys, q_back, q_away = tie(*keys, q_back, q_away)
    lifted = lift(scalars, segment_ordering, keys, latent_up_weight)
    (relayed,) = attend((far,), scalars, segment_ordering, [q_far], lifted)
    got = turn(relayed, 1)
    direct, mine = attend((back, away), scalars, segment_ordering, [q_back, q_away], lifted)
    direct = turn(direct, -1)
    passed = turn(relay(got, mine), 1)
    (own,) = attend((near,), scalars, segment_ordering, [queries], lifted)
    return tuple(final(scalars, own, direct, passed, *pieces))


def solution(mesh):
    split = Mesh(mesh.devices.reshape(SIZES), AXES)
    ctx, tp = ("y", "x", "zh"), ("zl", "core")
    in_specs = (
        P(),
        P(ctx, tp),
        P(ctx + tp, None),
        P(ctx, tp),
        P(tp, None),
        P(tp, None),
        P(),
        P(),
        P(ctx, None),
        P(),
        P(None, tp),
    )
    out_specs = (P(ctx + tp, None), P(ctx, tp))
    return jax.shard_map(body, mesh=split, in_specs=in_specs, out_specs=out_specs, check_vma=False)
```
